128 devices in a mesh: dp: 32 (over y, z, core), expert: 4 (over x).
Axes of the slice: x: 4, y: 4, z: 4, core: 2. Of those that a mesh axis runs over, the one named last changes fastest.
Arguments:
- gradient: float32 [32, 576, 7168], P(None, 'dp', 'expert')
- momentum: float32 [32, 576, 7168], P(None, 'dp', 'expert')
- owner_table: int32 [32], replicated, may hold values from 0 to 31, as said below
- shape_class: int32 [32], replicated, may hold values from 0 to 1
Outputs:
- new_moment: float32 [32, 576, 7168], P(None, 'dp', 'expert')
- update_rows: bfloat16 [32, 576, 7168], P(None, 'dp', 'expert')
- owned_update: bfloat16 [32, 576, 7168], P('dp', None, 'expert')
The draws below stay inside these ranges and needn't reach their ends.
Inputs may be any that keep to these rules, and one draw needn't show every extreme that they name: owner_table is a permutation: every dp index owns exactly one matrix.
All inputs are finite; a program needn't handle non-finite values.
Results may differ from the reference program's by a relative error of at most 0.012.
The reference program's roundings to bfloat16 on the way count: a program that leaves them out, or rounds other values in their place, can miss the bound.
Values may be sent and summed in bfloat16 or wider, within the bound.
A program may use at most 128 MiB of HBM per device.

```python
import math
import jax
import jax.numpy as jnp
from jax import lax

COLS = 7168
ROWS = 576
ROUTER_ROWS = 384
ITERS = 4
RDEV = 18
CDEV = 1792
MATS = 32
N_DP = 32


def draw_gradient(key, part):
    key = jax.random.fold_in(key, 11)
    keys = jax.random.split(key, 9)
    shape = (MATS, ROWS, COLS)
    row_ids = jnp.arange(ROWS, dtype=jnp.float32)[None, :, None]
    matrix_factor = jnp.exp(jax.random.uniform(keys[4], (MATS, 1, 1), jnp.float32, -1.5, 1.5))
    block_draw = jnp.exp(jax.random.uniform(keys[5], (1, ROWS // RDEV, 1), jnp.float32, -1.0, 1.0))
    block_factor = jnp.repeat(block_draw, RDEV, axis=1)
    row_scale = 10.0 ** (row_ids / ROWS) * jnp.exp(jax.random.uniform(keys[1], (MATS, ROWS, 1), jnp.float32) * jnp.log(2.0))
    column_scale = jnp.exp(jax.random.uniform(keys[2], (1, 1, COLS), jnp.float32) * jnp.log(10.0))
    quarter = jax.random.randint(keys[6], (MATS, 1, 1), 0, COLS // CDEV)
    column_ids = jnp.arange(COLS, dtype=jnp.int32)[None, None, :]
    focus = jnp.where(column_ids // CDEV == quarter, 3.0, 0.3).astype(jnp.float32)
    left_part = jax.random.normal(keys[7], (MATS, ROWS, 1), jnp.float32)
    right_part = jax.random.normal(keys[8], (MATS, 1, COLS), jnp.float32) * focus
    base = jax.random.normal(keys[0], shape, jnp.float32)
    mixed = base * column_scale + 6.0 * left_part * right_part
    return (mixed * matrix_factor * block_factor * row_scale).astype(jnp.float32)


def draw_momentum(key, part):
    key = jax.random.fold_in(key, 31)
    first, second = jax.random.split(key, 2)
    values = jax.random.truncated_normal(first, -6.0, 6.0, (MATS, ROWS, COLS), jnp.float32)
    matrix_factor = jnp.exp(jax.random.uniform(second, (MATS, 1, 1), jnp.float32, -1.0, 1.0))
    return (values * matrix_factor).astype(jnp.float32)


def draw_owner_table(key, part):
    key = jax.random.fold_in(key, 23)
    return jax.random.permutation(key, N_DP).astype(jnp.int32)


def touch_ends(values, stream_key, low, top_value):
    dims = values.shape
    index_at = [jax.random.randint(jax.random.fold_in(stream_key, axis), (), 0, dims[axis]) for axis in range(len(dims))]
    values = values.at[tuple(index_at)].set(low)
    longest = dims.index(max(dims))
    index_at[longest] = (index_at[longest] + 1) % dims[longest]
    return values.at[tuple(index_at)].set(top_value)


def setup_inputs(seed: int = 0) -> dict:
    arg_keys = jax.random.split(jax.random.key(seed), 5)
    return {
        "gradient": draw_gradient(jax.random.fold_in(arg_keys[4], 71), 0),
        "momentum": draw_momentum(jax.random.fold_in(arg_keys[4], 71), 0),
        "owner_table": draw_owner_table(jax.random.fold_in(arg_keys[4], 71), 0),
        "shape_class": touch_ends(jax.random.randint(arg_keys[3], (MATS,), 0, 2), jax.random.fold_in(arg_keys[3], 1), 0, 1).astype(jnp.int32),
    }


MU_RATE = 0.95
EPSILON = 1e-07
COEF_A = 3.4445
COEF_B = -4.775
COEF_C = 2.0315

def orthogonalize(matrix):
    current = matrix
    result = None
    for turn_index in range(ITERS):
        gram = jnp.dot(current, current.T, preferred_element_type=jnp.float32).astype(jnp.bfloat16)
        square = jnp.dot(gram, gram, preferred_element_type=jnp.float32)
        poly = (COEF_B * gram.astype(jnp.float32) + COEF_C * square).astype(jnp.bfloat16)
        result = COEF_A * current.astype(jnp.float32) + jnp.dot(poly, current, preferred_element_type=jnp.float32)
        if turn_index + 1 < ITERS:
            current = result.astype(jnp.bfloat16)
    return (0.2 * math.sqrt(COLS) * result).astype(jnp.bfloat16)

def reference(gradient, momentum, owner_table, shape_class):
    row_ids = jnp.arange(ROWS, dtype=jnp.int32)
    live = ((shape_class[:, None] == 0) | (row_ids[None, :] < ROUTER_ROWS)).astype(jnp.float32)[:, :, None]
    masked_grad = gradient * live
    masked_moment = momentum * live
    total = jnp.sum(masked_grad * masked_grad)
    clip = jnp.minimum(jnp.float32(1.0), jnp.sqrt(jnp.float32(MATS * ROWS * COLS) / total))
    new_moment = MU_RATE * masked_moment + clip * masked_grad
    blended = clip * masked_grad + MU_RATE * new_moment
    norm_m = jnp.sqrt(lax.optimization_barrier(jnp.sum(blended * blended, axis=(1, 2))))
    start = (blended / (norm_m + EPSILON)[:, None, None]).astype(jnp.bfloat16)
    update_rows = lax.map(orthogonalize, start)
    selected = (owner_table[None, :] == jnp.arange(N_DP, dtype=jnp.int32)[:, None]).astype(jnp.int32)
    position = lax.optimization_barrier(jnp.sum(selected * jnp.arange(MATS, dtype=jnp.int32)[None, :], axis=1)).astype(jnp.int32)
    owned_update = update_rows[position]
    return (new_moment, update_rows, owned_update)
```

```python
import functools
import math

import jax
import jax.numpy as jnp
from jax import lax
from jax.experimental import pallas as pl
from jax.experimental.pallas import tpu as pltpu
from jax.sharding import PartitionSpec as P

MESH = pl.DeviceIdType.MESH
F32, BF16 = jnp.float32, jnp.bfloat16
ROWS, COLS, MATS, RDEV, CDEV = 576, 7168, 32, 18, 1792
ROUTER_ROWS = 384
LOADS = 6
MU_RATE, EPSILON = 0.95, 1e-07
VMEM_LIMIT = 56 * 1024 * 1024


def place():
    dp = lax.axis_index("dp")
    return dp, lax.axis_index("expert"), dp // 8, (dp // 2) % 4, dp % 2


def shifted(y, z, c, j):
    return (((y + j // 8) % 4) * 4 + (z + (j // 2) % 4) % 4) * 2 + (c + j % 2) % 2


def gather_kernel(owner_s, cls_s, g_hbm, m_hbm, x_ref, nm_hbm,
                  g, m, nm, zs, perm, zmain, zlo, lor, ar1, ar2,
                  in_sem, out_sem, s1, r1, s2, r2, sm, rm, sl, rl):
    dp, ex, y, z, c = place()
    per = ROWS // LOADS
    loads = []
    for k in range(LOADS):
        rows = pl.ds(k * per, per)
        for n, (src, dst) in enumerate(((g_hbm, g), (m_hbm, m))):
            cp = pltpu.make_async_copy(src.at[rows], dst.at[rows], in_sem.at[n, k])
            cp.start()
            loads.append(cp)

    barrier = pltpu.get_barrier_semaphore()

    def greet(j, _):
        pl.semaphore_signal(barrier, inc=1, device_id=(shifted(y, z, c, j), ex), device_id_type=MESH)
        return _
    lax.fori_loop(1, 32, greet, 0)

    def greet_x(j, _):
        zz, xx = (z + j % 4) % 4, (ex + j // 4) % 4
        pl.semaphore_signal(barrier, inc=1, device_id=((y * 4 + zz) * 2 + c, xx), device_id_type=MESH)
        return _
    lax.fori_loop(4, 16, greet_x, 0)

    lane = lax.broadcasted_iota(jnp.int32, (8, ROWS), 1)
    owner_row = jnp.zeros((8, ROWS), jnp.int32)
    mat = lax.broadcasted_iota(jnp.int32, (MATS, 128), 0)
    cls = jnp.zeros((MATS, 128), F32)
    for i in range(MATS):
        owner_row = jnp.where(lane % MATS == i, owner_s[i], owner_row)
        cls = jnp.where(mat == i, cls_s[i].astype(F32), cls)
    wanted = owner_row * RDEV + lane // MATS
    for k in range(ROWS // 32):
        o = lax.broadcasted_iota(jnp.int32, (32, ROWS), 0) + 32 * k
        if k < 16:
            key = (o // 16) * RDEV + o % 16
        else:
            key = ((o - 512) // 2) * RDEV + 16 + o % 2
        perm[32 * k:32 * (k + 1), :] = (key == wanted[0:1]).astype(F32).astype(BF16)

    def live_at(r):
        return jnp.where(dp * RDEV + r < ROUTER_ROWS, 1.0, 1.0 - cls)

    def stats(r, acc):
        live = live_at(r)
        rows = pl.ds(pl.multiple_of(r * MATS, MATS), MATS)
        gg, gm, mm = acc
        for t in range(CDEV // 128):
            gv = g[rows, t * 128:(t + 1) * 128] * live
            mv = m[rows, t * 128:(t + 1) * 128] * live
            mv = mv * (MU_RATE * MU_RATE)
            gg, gm, mm = gg + gv * gv, gm + gv * mv, mm + mv * mv
        return gg, gm, mm

    zero = jnp.zeros((MATS, 128), F32)
    acc = (zero, zero, zero)
    for k in range(LOADS):
        loads[2 * k].wait()
        loads[2 * k + 1].wait()
        acc = lax.fori_loop(k * (RDEV // LOADS), (k + 1) * (RDEV // LOADS), stats, acc)
    sums = [jnp.sum(a, axis=1, keepdims=True) for a in acc]
    col = lax.broadcasted_iota(jnp.int32, (MATS, 128), 1)
    mine = jnp.where(col == 0, sums[0], jnp.where(col == 1, sums[1], jnp.where(col == 2, sums[2], 0.0)))

    pl.semaphore_wait(barrier, 31 + 12)

    i1, i2 = y * 2 + c, ex * 4 + z
    ar1[i1] = mine

    def first_of(j):
        return (y + j // 2) % 4, (c + j % 2) % 2

    def first(j):
        yy, cc = first_of(j)
        return pltpu.make_async_remote_copy(
            src_ref=ar1.at[i1], dst_ref=ar1.at[i1], send_sem=s1.at[j], recv_sem=r1.at[i1],
            device_id=((yy * 4 + z) * 2 + cc, ex), device_id_type=MESH)

    def got(buf, slot, sem):
        return pltpu.make_async_copy(buf.at[slot], buf.at[slot], sem.at[slot])

    for j in range(1, 8):
        first(j).start()
    for j in range(1, 8):
        yy, cc = first_of(j)
        got(ar1, yy * 2 + cc, r1).wait()
    ar2[i2] = jnp.sum(ar1[...], axis=0)

    def second_of(j):
        return (z + j % 4) % 4, (ex + j // 4) % 4

    def second(j):
        zz, xx = second_of(j)
        return pltpu.make_async_remote_copy(
            src_ref=ar2.at[i2], dst_ref=ar2.at[i2], send_sem=s2.at[j], recv_sem=r2.at[i2],
            device_id=((y * 4 + zz) * 2 + c, xx), device_id_type=MESH)

    for j in range(1, 16):
        second(j).start()
    for j in range(1, 16):
        zz, xx = second_of(j)
        got(ar2, xx * 4 + zz, r2).wait()
    tot = jnp.sum(ar2[...], axis=0)
    gg, gm, mm = tot[:, 0:1], tot[:, 1:2], tot[:, 2:3]
    total = jnp.sum(gg, axis=0, keepdims=True)
    clip = jnp.minimum(1.0, jnp.sqrt(float(MATS * ROWS * COLS) / total))
    rate = (1.0 + MU_RATE) * clip
    sq = jnp.where(clip > 0.0, rate * rate * gg + 2.0 * rate * gm, 0.0) + mm
    norm = jnp.sqrt(jnp.maximum(sq, 0.0))
    inv = jnp.broadcast_to(1.0 / (norm + EPSILON), (MATS, 128))
    clip = jnp.broadcast_to(clip, (MATS, 128))

    def blend(r, _):
        live = live_at(r)
        lc = live * clip
        lm = live * MU_RATE
        rows = pl.ds(pl.multiple_of(r * MATS, MATS), MATS)
        for t in range(CDEV // 128):
            cols = slice(t * 128, (t + 1) * 128)
            gv = g[rows, cols] * lc
            nv = m[rows, cols] * lm + gv
            nm[rows, cols] = nv
            zs[rows, cols] = ((gv + MU_RATE * nv) * inv).astype(BF16)
        return _
    lax.fori_loop(0, RDEV, blend, 0)

    save = pltpu.make_async_copy(nm, nm_hbm, out_sem)
    save.start()

    for t in range(CDEV // 256):
        cols = slice(t * 256, (t + 1) * 256)
        out = jnp.dot(perm[...], zs[:, cols], preferred_element_type=F32)
        zmain[:, cols] = out[:512].astype(BF16)
        zlo[:, :, cols] = out[512:].reshape(MATS, 2, 256).astype(BF16)

    def block(ref, i):
        return ref.at[pl.ds(pl.multiple_of(i * 16, 16), 16)]

    def main_copy(j):
        to = shifted(y, z, c, j)
        return pltpu.make_async_remote_copy(
            src_ref=block(zmain, to), dst_ref=block(x_ref, dp), send_sem=sm.at[j], recv_sem=rm.at[dp],
            device_id=(to, ex), device_id_type=MESH)

    def lo_copy(j):
        to = shifted(y, z, c, j)
        return pltpu.make_async_remote_copy(
            src_ref=zlo.at[to], dst_ref=lor.at[dp], send_sem=sl.at[j], recv_sem=rl.at[dp],
            device_id=(to, ex), device_id_type=MESH)

    def send(j, _):
        main_copy(j).start()
        lo_copy(j).start()
        return _
    lax.fori_loop(1, 32, send, 0)
    own = pl.ds(pl.multiple_of(dp * 16, 16), 16)
    x_ref[own, :] = zmain[own, :]
    lor[dp] = zlo[dp]

    def receive(j, _):
        frm = shifted(y, z, c, j)
        pltpu.make_async_copy(block(x_ref, frm), block(x_ref, frm), rm.at[frm]).wait()
        pltpu.make_async_copy(lor.at[frm], lor.at[frm], rl.at[frm]).wait()
        return _
    lax.fori_loop(1, 32, receive, 0)
    x_ref[512:, :] = lor[...].astype(F32).reshape(64, CDEV).astype(BF16)

    def sent(j, _):
        main_copy(j).wait_send()
        lo_copy(j).wait_send()
        return _
    lax.fori_loop(1, 32, sent, 0)
    for j in range(1, 8):
        first(j).wait_send()
    for j in range(1, 16):
        second(j).wait_send()
    save.wait()


def gather_rows(owner, cls, g, m):
    D = pltpu.SemaphoreType.DMA
    return pl.pallas_call(
        gather_kernel,
        out_shape=(jax.ShapeDtypeStruct((ROWS, CDEV), BF16), jax.ShapeDtypeStruct((ROWS, CDEV), F32)),
        in_specs=[pl.BlockSpec(memory_space=pltpu.SMEM)] * 2 + [pl.BlockSpec(memory_space=pl.ANY)] * 2,
        out_specs=(pl.BlockSpec(memory_space=pltpu.VMEM), pl.BlockSpec(memory_space=pl.ANY)),
        scratch_shapes=[
            pltpu.VMEM((ROWS, CDEV), F32), pltpu.VMEM((ROWS, CDEV), F32), pltpu.VMEM((ROWS, CDEV), F32),
            pltpu.VMEM((ROWS, CDEV), BF16), pltpu.VMEM((ROWS, ROWS), BF16),
            pltpu.VMEM((512, CDEV), BF16), pltpu.VMEM((MATS, 2, CDEV), BF16), pltpu.VMEM((MATS, 2, CDEV), BF16),
            pltpu.VMEM((8, MATS, 128), F32), pltpu.VMEM((16, MATS, 128), F32),
            D((2, LOADS)), D, D((8,)), D((8,)), D((16,)), D((16,)), D((32,)), D((32,)), D((32,)), D((32,)),
        ],
        compiler_params=pltpu.CompilerParams(collective_id=0, has_side_effects=True, vmem_limit_bytes=VMEM_LIMIT),
    )(owner, cls, g, m)


COEF_A, COEF_B, COEF_C, ITERS = 3.4445, -4.775, 2.0315, 4
SCALE = 0.2 * math.sqrt(COLS)
CHUNK = 256
QUARTER = 7
PANELS = [(r, t) for r in range(9) for t in range(r // 2 + 1)]


def dot(a, b):
    return jnp.dot(a, b, preferred_element_type=F32)


def dot_t(a, b):
    return lax.dot_general(a, b, (((1,), (1,)), ((), ())), preferred_element_type=F32)


def slot_key(o):
    return jnp.where(o < 512, (o // 16) * RDEV + o % 16, ((o - 512) // 2) * RDEV + 16 + o % 2)


def halving_places(ex, c):
    near = ex + 1 - 2 * (ex % 2)
    far = 3 - ex
    first = (1 - c) * near + c * far
    second = (1 - c) * far + c * near

    def part(x):
        h = (1 - c) * (((x + 1) // 2) % 2) + c * (x // 2)
        q = (1 - c) * (x // 2) + c * (x % 2)
        return h, q
    return first, second, part


def update_kernel(owner_s, x_ref, up_ref, own_ref,
                  part, got1, got2, full, gram, t_ref, coef, u, ulo, vmain, vlo, v, perm, order,
                  xs, xr, sm, rm, sl, rl):
    dp, ex, y, z, c = place()
    first, second, part_of = halving_places(ex, c)
    h, q = part_of(ex)
    h1, q1 = part_of(first)

    barrier = pltpu.get_barrier_semaphore()

    def greet(j, _):
        pl.semaphore_signal(barrier, inc=1, device_id=(shifted(y, z, c, j), ex), device_id_type=MESH)
        return _
    lax.fori_loop(1, 32, greet, 0)
    for other in (first, second):
        pl.semaphore_signal(barrier, inc=1, device_id=(dp, other), device_id_type=MESH)

    for lo, hi in ((0, 256), (256, 512), (512, 576)):
        block = dot_t(x_ref[lo:, :], x_ref[lo:hi, :])
        for n, (r, t) in enumerate(PANELS):
            if lo <= 128 * t < hi:
                w = min(128, hi - 128 * t)
                piece = block[64 * r - lo:64 * r - lo + 64, 128 * t - lo:128 * t - lo + w]
                if w < 128:
                    piece = jnp.concatenate([piece, jnp.zeros((64, 128 - w), F32)], axis=1)
                part[n] = piece
    for n in range(len(PANELS), 4 * QUARTER):
        part[n] = jnp.zeros((64, 128), F32)

    pl.semaphore_wait(barrier, 33)

    def panels(ref, hh, qq):
        return ref.at[pl.ds((2 * hh + qq) * QUARTER, QUARTER)]

    def exchange(src, dst, n, to):
        return pltpu.make_async_remote_copy(
            src_ref=src, dst_ref=dst, send_sem=xs.at[n], recv_sem=xr.at[n],
            device_id=(dp, to), device_id_type=MESH)

    a1 = exchange(panels(part, h1, 1 - q1), got1.at[0], 0, first)
    a2 = exchange(panels(part, h1, q1), got1.at[1], 1, first)
    a1.start()
    a2.start()
    a1.wait_recv()
    pass_on, keep = pl.ds((2 * h + 1 - q) * QUARTER, QUARTER), pl.ds((2 * h + q) * QUARTER, QUARTER)
    part[pass_on] = part[pass_on] + got1[0]
    b = exchange(panels(part, h, 1 - q), got2, 2, second)
    b.start()
    a2.wait_recv()
    kept = part[keep] + got1[1]
    part[keep] = kept
    b.wait_recv()
    full[keep] = part[keep] + got2[...]
    c1 = exchange(panels(full, h, q), panels(full, h, q), 3, second)
    c2 = exchange(panels(full, h, q), panels(full, h, q), 4, first)
    c1.start()
    c2.start()
    c1.wait_recv()
    c3 = exchange(panels(full, h, 1 - q), panels(full, h, 1 - q), 5, first)
    c3.start()

    mat = lax.broadcasted_iota(jnp.int32, (MATS, ROWS), 0)
    owner_col = jnp.zeros((MATS, ROWS), jnp.int32)
    for i in range(MATS):
        owner_col = jnp.where(mat == i, owner_s[i], owner_col)
    key = slot_key(lax.broadcasted_iota(jnp.int32, (MATS, ROWS), 1))
    for r in range(RDEV):
        rows = slice(MATS * r, MATS * (r + 1))
        perm[rows, :] = (owner_col * RDEV + r == key).astype(F32).astype(BF16)
        order[rows, :] = (mat + MATS * r == key).astype(F32).astype(BF16)

    c2.wait_recv()
    c3.wait_recv()

    for n, (r, t) in enumerate(PANELS):
        w = min(128, ROWS - 128 * t)
        piece = full[n]
        gram[64 * r:64 * r + 64, 128 * t:128 * t + w] = piece[:, :w]
        if t < r // 2:
            gram[128 * t:128 * t + 128, 64 * r:64 * r + 64] = piece.T

    for k in range(ITERS):
        a16 = gram[...].astype(BF16)
        b16 = (COEF_B * a16.astype(F32) + COEF_C * dot(a16, a16)).astype(BF16)
        coef[k] = b16
        if k + 1 < ITERS:
            low = (gram[...] - a16.astype(F32)).astype(BF16)
            t_ref[...] = COEF_A * gram[...] + (dot(a16, b16) + dot(low, b16))
            t16 = t_ref[...].astype(BF16)
            tlow = (t_ref[...] - t16.astype(F32)).astype(BF16)
            gram[...] = COEF_A * t_ref[...] + (dot(b16, t16) + dot(b16, tlow))

    def block(ref, i):
        return ref.at[pl.ds(pl.multiple_of(i * 16, 16), 16)]

    def main_copy(j):
        to = shifted(y, z, c, j)
        return pltpu.make_async_remote_copy(
            src_ref=block(u, to), dst_ref=block(vmain, dp), send_sem=sm.at[j], recv_sem=rm.at[dp],
            device_id=(to, ex), device_id_type=MESH)

    def lo_copy(j):
        to = shifted(y, z, c, j)
        return pltpu.make_async_remote_copy(
            src_ref=ulo.at[to], dst_ref=vlo.at[dp], send_sem=sl.at[j], recv_sem=rl.at[dp],
            device_id=(to, ex), device_id_type=MESH)

    for n in range(CDEV // CHUNK):
        cols = slice(n * CHUNK, (n + 1) * CHUNK)
        cur = x_ref[:, cols]
        for k in range(ITERS):
            out = COEF_A * cur.astype(F32) + dot(coef[k], cur)
            if k + 1 < ITERS:
                cur = out.astype(BF16)
        res = (SCALE * out).astype(BF16)
        u[:, cols] = res
        ulo[:, :, cols] = res[512:].astype(F32).reshape(MATS, 2, CHUNK).astype(BF16)

    def send(j, _):
        main_copy(j).start()
        lo_copy(j).start()
        return _
    lax.fori_loop(1, 32, send, 0)

    own = pl.ds(pl.multiple_of(dp * 16, 16), 16)
    vmain[own, :] = u[own, :]
    vlo[dp] = ulo[dp]

    for n in range(CDEV // CHUNK):
        cols = slice(n * CHUNK, (n + 1) * CHUNK)
        own_ref[:, cols] = dot(order[...], u[:, cols]).astype(BF16)

    def receive(j, _):
        frm = shifted(y, z, c, j)
        pltpu.make_async_copy(block(vmain, frm), block(vmain, frm), rm.at[frm]).wait()
        pltpu.make_async_copy(vlo.at[frm], vlo.at[frm], rl.at[frm]).wait()
        return _
    lax.fori_loop(1, 32, receive, 0)
    v[...] = vlo[...].astype(F32).reshape(64, CDEV).astype(BF16)
    for n in range(CDEV // CHUNK):
        cols = slice(n * CHUNK, (n + 1) * CHUNK)
        up_ref[:, cols] = (dot(perm[:, :512], vmain[:, cols]) + dot(perm[:, 512:], v[:, cols])).astype(BF16)

    def sent(j, _):
        main_copy(j).wait_send()
        lo_copy(j).wait_send()
        return _
    lax.fori_loop(1, 32, sent, 0)
    for cp in (a1, a2, b, c1, c2, c3):
        cp.wait_send()


def update_rows_of(owner, x):
    D = pltpu.SemaphoreType.DMA
    V = pltpu.VMEM
    return pl.pallas_call(
        update_kernel,
        out_shape=(jax.ShapeDtypeStruct((ROWS, CDEV), BF16),) * 2,
        in_specs=[pl.BlockSpec(memory_space=pltpu.SMEM), pl.BlockSpec(memory_space=pltpu.VMEM)],
        out_specs=(pl.BlockSpec(memory_space=pltpu.VMEM),) * 2,
        scratch_shapes=[
            V((4 * QUARTER, 64, 128), F32), V((2, QUARTER, 64, 128), F32), V((QUARTER, 64, 128), F32),
            V((4 * QUARTER, 64, 128), F32), V((ROWS, ROWS), F32), V((ROWS, ROWS), F32), V((ITERS, ROWS, ROWS), BF16),
            V((ROWS, CDEV), BF16), V((MATS, 2, CDEV), BF16), V((512, CDEV), BF16), V((MATS, 2, CDEV), BF16),
            V((64, CDEV), BF16), V((ROWS, ROWS), BF16), V((ROWS, ROWS), BF16),
            D((6,)), D((6,)), D((32,)), D((32,)), D((32,)), D((32,)),
        ],
        compiler_params=pltpu.CompilerParams(collective_id=1, has_side_effects=True, vmem_limit_bytes=VMEM_LIMIT),
    )(owner, x)


def body(gradient, momentum, owner_table, shape_class):
    g = jnp.transpose(gradient, (1, 0, 2)).reshape(ROWS, CDEV)
    m = jnp.transpose(momentum, (1, 0, 2)).reshape(ROWS, CDEV)
    x, nm = gather_rows(owner_table, shape_class, g, m)
    up, own = update_rows_of(owner_table, x)
    new_moment = jnp.transpose(nm.reshape(RDEV, MATS, CDEV), (1, 0, 2))
    update = jnp.transpose(up.reshape(RDEV, MATS, CDEV), (1, 0, 2))
    return new_moment, update, own[None]


def solution(mesh):
    return jax.shard_map(
        body,
        mesh=mesh,
        in_specs=(P(None, "dp", "expert"), P(None, "dp", "expert"), P(), P()),
        out_specs=(P(None, "dp", "expert"), P(None, "dp", "expert"), P("dp", None, "expert")),
        check_vma=False,
    )
```

```python
import math

import jax
import jax.numpy as jnp
from jax import lax
from jax.experimental import pallas as pl
from jax.experimental.pallas import tpu as pltpu
from jax.sharding import PartitionSpec as P

MESH = pl.DeviceIdType.MESH
F32, BF16 = jnp.float32, jnp.bfloat16
ROWS, COLS, MATS, RDEV, CDEV = 576, 7168, 32, 18, 1792
ROUTER_ROWS = 384
LOADS = 6
MU_RATE, EPSILON = 0.95, 1e-07
COEF_A, COEF_B, COEF_C, ITERS = 3.4445, -4.775, 2.0315, 4
SCALE = 0.2 * math.sqrt(COLS)
VMEM_LIMIT = 58 * 1024 * 1024
EARLY = 24
MAIN = 512
OUT_PARTS = ((0, 256), (256, 768), (768, CDEV))
FIRST = [(r, t) for r in range(7) for t in range(r // 2 + 1)]
LAST = [(r, t) for r in (7, 8) for t in range(r // 2 + 1)]
Q_FIRST, Q_LAST = 8, 5


def dot(a, b):
    return jnp.dot(a, b, preferred_element_type=F32)


def dot_t(a, b):
    return lax.dot_general(a, b, (((1,), (1,)), ((), ())), preferred_element_type=F32)


def away(n):
    late = n // 16
    dy = (1 - late) * 2 * (n // 8) + late * (1 + 2 * ((n % 8) // 4))
    dz = (1 - late) * ((n // 2) % 4) + late * (2 * ((n // 2) % 2) + n // EARLY)
    return dy, dz, n % 2


def one_hot(match):
    return match.astype(F32).astype(BF16)


def halving_places(ex, c):
    near = ex + 1 - 2 * (ex % 2)
    far = 3 - ex
    first = (1 - c) * near + c * far
    second = (1 - c) * far + c * near

    def part(x):
        h = (1 - c) * (((x + 1) // 2) % 2) + c * (x // 2)
        q = (1 - c) * (x // 2) + c * (x % 2)
        return h, q
    return first, second, part


def kernel(owner_s, cls_s, g_hbm, m_hbm, nm_hbm, up_hbm, own_hbm,
           g, m, nm, zs, zmain, zlo, lor, x, ar1, ar2,
           perm_m, perm_l, back_m, back_l, order,
           part1, part2, got1a, got1b, got2a, got2b, full1, full2, gram, t_ref, coef,
           u, ulo, vmain, vlo, vl, up, own,
           in_sem, nm_sem, own_sem, up_sem, s1, r1, s2, r2, sm, rm, sl, rl, so, ro, slo, rlo, xs, xr):
    dp, ex = lax.axis_index("dp"), lax.axis_index("expert")
    y, z, c = dp // 8, (dp // 2) % 4, dp % 2

    def ahead(n):
        dy, dz, dc = away(n)
        return (((y + dy) % 4) * 4 + (z + dz) % 4) * 2 + (c + dc) % 2

    def behind(n):
        dy, dz, dc = away(n)
        return (((y + 4 - dy) % 4) * 4 + (z + 4 - dz) % 4) * 2 + (c + dc) % 2

    per = ROWS // LOADS
    loads = []
    for k in range(LOADS):
        rows = pl.ds(k * per, per)
        for n, (src, dst) in enumerate(((g_hbm, g), (m_hbm, m))):
            cp = pltpu.make_async_copy(src.at[rows], dst.at[rows], in_sem.at[n, k])
            cp.start()
            loads.append(cp)

    barrier = pltpu.get_barrier_semaphore()

    def greet(j, _):
        pl.semaphore_signal(barrier, inc=1, device_id=(ahead(j), ex), device_id_type=MESH)
        return _
    lax.fori_loop(1, 32, greet, 0)

    def greet_x(j, _):
        zz, xx = (z + j % 4) % 4, (ex + j // 4) % 4
        pl.semaphore_signal(barrier, inc=1, device_id=((y * 4 + zz) * 2 + c, xx), device_id_type=MESH)
        return _
    lax.fori_loop(4, 16, greet_x, 0)

    lane = lax.broadcasted_iota(jnp.int32, (8, ROWS), 1)
    mat = lax.broadcasted_iota(jnp.int32, (MATS, 128), 0)
    owner_row = jnp.zeros((8, ROWS), jnp.int32)
    cls = jnp.zeros((MATS, 128), F32)
    for i in range(MATS):
        owner_row = jnp.where(lane % MATS == i, owner_s[i], owner_row)
        cls = jnp.where(mat == i, cls_s[i].astype(F32), cls)
    wanted = (owner_row * RDEV + lane // MATS)[0:1]
    for k in range(16):
        o = lax.broadcasted_iota(jnp.int32, (32, MAIN), 0) + 32 * k
        perm_m[32 * k:32 * (k + 1), :] = one_hot((o // 16) * RDEV + o % 16 == wanted[:, :MAIN])
    o = lax.broadcasted_iota(jnp.int32, (64, 64), 0)
    perm_l[...] = one_hot((o // 2) * RDEV + 16 + o % 2 == wanted[:, MAIN:])

    def live_at(r):
        return jnp.where(dp * RDEV + r < ROUTER_ROWS, 1.0, 1.0 - cls)

    def rows_of(r):
        return pl.ds(pl.multiple_of(r * MATS, MATS), MATS)

    def stats(r, acc):
        live = live_at(r)
        gg, gm, mm = acc
        for t in range(CDEV // 128):
            cols = slice(t * 128, (t + 1) * 128)
            gv = g[rows_of(r), cols] * live
            mv = m[rows_of(r), cols] * (live * (MU_RATE * MU_RATE))
            gg, gm, mm = gg + gv * gv, gm + gv * mv, mm + mv * mv
        return gg, gm, mm

    acc = (jnp.zeros((MATS, 128), F32),) * 3
    for k in range(LOADS):
        loads[2 * k].wait()
        loads[2 * k + 1].wait()
        acc = lax.fori_loop(k * (RDEV // LOADS), (k + 1) * (RDEV // LOADS), stats, acc)
    sums = [jnp.sum(a, axis=1, keepdims=True) for a in acc]
    col = lax.broadcasted_iota(jnp.int32, (MATS, 128), 1)
    mine = jnp.where(col == 0, sums[0], jnp.where(col == 1, sums[1], jnp.where(col == 2, sums[2], 0.0)))
    mine = jnp.concatenate([mine, jnp.zeros((128 - MATS, 128), F32)], axis=0).T[:8]

    pl.semaphore_wait(barrier, 31 + 12)

    i1, i2 = y * 2 + c, ex * 4 + z
    ar1[i1] = mine

    def got(buf, slot, sem):
        return pltpu.make_async_copy(buf.at[slot], buf.at[slot], sem.at[slot])

    def one_of(j):
        return (y + j // 2) % 4, (c + j % 2) % 2

    def one(j):
        yy, cc = one_of(j)
        return pltpu.make_async_remote_copy(
            src_ref=ar1.at[i1], dst_ref=ar1.at[i1], send_sem=s1.at[j], recv_sem=r1.at[i1],
            device_id=((yy * 4 + z) * 2 + cc, ex), device_id_type=MESH)

    def two_of(j):
        return (z + j % 4) % 4, (ex + j // 4) % 4

    def two(j):
        zz, xx = two_of(j)
        return pltpu.make_async_remote_copy(
            src_ref=ar2.at[i2], dst_ref=ar2.at[i2], send_sem=s2.at[j], recv_sem=r2.at[i2],
            device_id=((y * 4 + zz) * 2 + c, xx), device_id_type=MESH)

    for j in range(1, 8):
        one(j).start()
    for j in range(1, 8):
        yy, cc = one_of(j)
        got(ar1, yy * 2 + cc, r1).wait()
    ar2[i2] = jnp.sum(ar1[...], axis=0)
    for j in range(1, 16):
        two(j).start()
    for j in range(1, 16):
        zz, xx = two_of(j)
        got(ar2, xx * 4 + zz, r2).wait()
    tot = jnp.concatenate([jnp.sum(ar2[...], axis=0), jnp.zeros((120, 128), F32)], axis=0).T[:MATS]
    gg, gm, mm = tot[:, 0:1], tot[:, 1:2], tot[:, 2:3]
    total = jnp.sum(gg, axis=0, keepdims=True)
    clip = jnp.minimum(1.0, jnp.sqrt(float(MATS * ROWS * COLS) / total))
    rate = (1.0 + MU_RATE) * clip
    sq = jnp.where(clip > 0.0, rate * rate * gg + 2.0 * rate * gm, 0.0) + mm
    norm = jnp.sqrt(jnp.maximum(sq, 0.0))
    inv = jnp.broadcast_to(1.0 / (norm + EPSILON), (MATS, 128))
    clip = jnp.broadcast_to(clip, (MATS, 128))

    def blend(r, _):
        live = live_at(r)
        lc = live * clip
        lm = live * MU_RATE
        for t in range(CDEV // 128):
            cols = slice(t * 128, (t + 1) * 128)
            gv = g[rows_of(r), cols] * lc
            nv = m[rows_of(r), cols] * lm + gv
            nm[rows_of(r), cols] = nv
            zs[rows_of(r), cols] = ((gv + MU_RATE * nv) * inv).astype(BF16)
        return _
    lax.fori_loop(0, RDEV, blend, 0)
    for t in range(CDEV // 256):
        cols = slice(t * 256, (t + 1) * 256)
        zmain[:, cols] = dot(perm_m[...], zs[:MAIN, cols]).astype(BF16)
        zlo[:, :, cols] = dot(perm_l[...], zs[MAIN:, cols]).reshape(MATS, 2, 256).astype(BF16)

    def block(ref, i):
        return ref.at[pl.ds(pl.multiple_of(i * 16, 16), 16)]

    def slot(ref, n):
        return block(ref, n + 4 * (n // EARLY))

    def main_in(n):
        to = ahead(n)
        return pltpu.make_async_remote_copy(
            src_ref=block(zmain, to), dst_ref=slot(x, n), send_sem=sm.at[n], recv_sem=rm.at[n],
            device_id=(to, ex), device_id_type=MESH)

    def lo_in(n):
        to = ahead(n)
        return pltpu.make_async_remote_copy(
            src_ref=zlo.at[to], dst_ref=lor.at[n], send_sem=sl.at[n], recv_sem=rl.at[n],
            device_id=(to, ex), device_id_type=MESH)

    def each(lo, hi, act):
        def step(n, _):
            act(n)
            return _
        lax.fori_loop(lo, hi, step, 0)

    each(1, 32, lambda n: lo_in(n).start())
    each(1, EARLY, lambda n: main_in(n).start())
    save_nm = pltpu.make_async_copy(nm, nm_hbm, nm_sem)
    save_nm.start()
    x[0:16, :] = zmain[pl.ds(pl.multiple_of(dp * 16, 16), 16), :]
    lor[0] = zlo[dp]

    owner_col = jnp.zeros((MATS, MAIN), jnp.int32)
    mats = lax.broadcasted_iota(jnp.int32, (MATS, MAIN), 0)
    for i in range(MATS):
        owner_col = jnp.where(mats == i, owner_s[i], owner_col)
    owner_col = owner_col * RDEV
    key = ((lane // 16) * RDEV + lane % 16)[0:1, :MAIN]
    for r in range(16):
        back_m[MATS * r:MATS * (r + 1), :] = one_hot(owner_col + r == key)
    key = ((lane // 2) * RDEV + 16 + lane % 2)[0:1, :64]
    for r in range(2):
        back_l[MATS * r:MATS * (r + 1), :] = one_hot(owner_col[:, :64] + (16 + r) == key)
    short = (lane >= 16 * EARLY) & (lane < 16 * EARLY + 64)
    n = jnp.where(short, (lane - 16 * EARLY) // 2, jnp.where(lane < 16 * EARLY, lane // 16, lane // 16 - 4))
    key = (behind(n) * RDEV + jnp.where(short, 16 + lane % 2, lane % 16))[0:1]
    for k in range(RDEV):
        rows = lax.broadcasted_iota(jnp.int32, (MATS, ROWS), 0) + MATS * k
        order[MATS * k:MATS * (k + 1), :] = one_hot(rows == key)

    each(1, EARLY, lambda n: main_in(n).wait_send())
    each(EARLY, 32, lambda n: main_in(n).start())

    def arrive(ref_at, sem, n):
        pltpu.make_async_copy(ref_at, ref_at, sem.at[n]).wait()

    each(1, EARLY, lambda n: arrive(slot(x, n), rm, n))
    each(1, 32, lambda n: arrive(lor.at[n], rl, n))
    x[16 * EARLY:16 * EARLY + 64, :] = lor[...].astype(F32).reshape(64, CDEV).astype(BF16)

    def put(part, n, piece):
        if piece.shape[1] < 128:
            piece = jnp.concatenate([piece, jnp.zeros((64, 128 - piece.shape[1]), F32)], axis=1)
        part[2 * n] = piece[:32]
        part[2 * n + 1] = piece[32:]

    top = 448
    for lo, hi in ((0, 256), (256, top)):
        gb = dot_t(x[lo:top, :], x[lo:hi, :])
        for n, (r, t) in enumerate(FIRST):
            if lo <= 128 * t < hi:
                put(part1, n, gb[64 * r - lo:64 * r - lo + 64, 128 * t - lo:min(128 * t + 128, hi) - lo])

    first, second, part_of = halving_places(ex, c)
    h, q = part_of(ex)
    h1, q1 = part_of(first)

    class Sum:
        def __init__(self, part, got_a, got_b, full, size, base):
            self.part, self.got_a, self.got_b, self.full, self.size, self.base = part, got_a, got_b, full, size, base

        def at(self, hh, qq):
            return pl.ds((2 * hh + qq) * self.size, self.size)

        def move(self, src, dst, n, to):
            return pltpu.make_async_remote_copy(
                src_ref=src, dst_ref=dst, send_sem=xs.at[self.base + n], recv_sem=xr.at[self.base + n],
                device_id=(dp, to), device_id_type=MESH)

        def halves(self):
            self.a1 = self.move(self.part.at[self.at(h1, 1 - q1)], self.got_a.at[0], 0, first)
            self.a2 = self.move(self.part.at[self.at(h1, q1)], self.got_a.at[1], 1, first)
            self.a1.start()
            self.a2.start()

        def quarters(self):
            self.a1.wait_recv()
            pass_on = self.at(h, 1 - q)
            self.part[pass_on] = self.part[pass_on] + self.got_a[0]
            self.b = self.move(self.part.at[pass_on], self.got_b, 2, second)
            self.b.start()

        def finish(self):
            self.a2.wait_recv()
            self.b.wait_recv()
            keep = self.at(h, q)
            self.full[keep] = self.part[keep] + self.got_a[1] + self.got_b[...]
            self.c1 = self.move(self.full.at[keep], self.full.at[keep], 3, second)
            self.c2 = self.move(self.full.at[keep], self.full.at[keep], 4, first)
            self.c1.start()
            self.c2.start()

        def forward(self):
            self.c1.wait_recv()
            other = self.at(h, 1 - q)
            self.c3 = self.move(self.full.at[other], self.full.at[other], 5, first)
            self.c3.start()

        def done(self):
            self.c2.wait_recv()
            self.c3.wait_recv()

        def sent(self):
            for cp in (self.a1, self.a2, self.b, self.c1, self.c2, self.c3):
                cp.wait_send()

    def lay_out(panels, full):
        for n, (r, t) in enumerate(panels):
            w = min(128, ROWS - 128 * t)
            piece = jnp.concatenate([full[2 * n], full[2 * n + 1]], axis=0)
            if 128 * t + 128 > top and r < 7:
                w = top - 128 * t
            gram[64 * r:64 * r + 64, 128 * t:128 * t + w] = piece[:, :w]
            if 128 * t + w <= 64 * r:
                gram[128 * t:128 * t + w, 64 * r:64 * r + 64] = piece.T[:w]
            elif 128 * t < 64 * r:
                gram[128 * t:64 * r, 64 * r:64 * r + 64] = piece.T[:64 * r - 128 * t]

    e1 = Sum(part1, got1a, got1b, full1, Q_FIRST, 0)
    e2 = Sum(part2, got2a, got2b, full2, Q_LAST, 6)
    e1.halves()
    e1.quarters()
    each(EARLY, 32, lambda n: arrive(slot(x, n), rm, n))
    gb = dot_t(x[top:, :], x[...])
    for n, (r, t) in enumerate(LAST):
        put(part2, n, gb[64 * r - top:64 * r - top + 64, 128 * t:min(128 * t + 128, ROWS)])
    for n in range(2 * len(LAST), 4 * Q_LAST):
        part2[n] = jnp.zeros((32, 128), F32)
    e2.halves()
    e1.finish()
    e2.quarters()
    e1.forward()
    e2.finish()
    e1.done()
    lay_out(FIRST, full1)
    e2.forward()
    e2.done()
    lay_out(LAST, full2)

    for k in range(ITERS):
        a16 = gram[...].astype(BF16)
        b16 = (COEF_B * a16.astype(F32) + COEF_C * dot(a16, a16)).astype(BF16)
        coef[k] = b16
        if k + 1 < ITERS:
            low = (gram[...] - a16.astype(F32)).astype(BF16)
            t_ref[...] = COEF_A * gram[...] + (dot(a16, b16) + dot(low, b16))
            t16 = t_ref[...].astype(BF16)
            tlow = (t_ref[...] - t16.astype(F32)).astype(BF16)
            gram[...] = COEF_A * t_ref[...] + (dot(b16, t16) + dot(b16, tlow))

    def main_out(p, n):
        to = behind(n)
        cols = pl.ds(OUT_PARTS[p][0], OUT_PARTS[p][1] - OUT_PARTS[p][0])
        return pltpu.make_async_remote_copy(
            src_ref=u.at[pl.ds(pl.multiple_of((n + 4 * (n // EARLY)) * 16, 16), 16), cols],
            dst_ref=vmain.at[pl.ds(pl.multiple_of(dp * 16, 16), 16), cols],
            send_sem=so.at[p, n], recv_sem=ro.at[p, n], device_id=(to, ex), device_id_type=MESH)

    def lo_out(n):
        to = behind(n)
        return pltpu.make_async_remote_copy(
            src_ref=ulo.at[n], dst_ref=vlo.at[dp], send_sem=slo.at[n], recv_sem=rlo.at[n],
            device_id=(to, ex), device_id_type=MESH)

    for p, (lo, hi) in enumerate(OUT_PARTS):
        for at in range(lo, hi, 512):
            cols = slice(at, min(at + 512, hi))
            cur = x[:, cols]
            for k in range(ITERS):
                out = COEF_A * cur.astype(F32) + dot(coef[k], cur)
                if k + 1 < ITERS:
                    cur = out.astype(BF16)
            res = (SCALE * out).astype(BF16)
            u[:, cols] = res
            ulo[:, :, cols] = res[16 * EARLY:16 * EARLY + 64].astype(F32).reshape(MATS, 2, cols.stop - at).astype(BF16)
        each(1, 32, lambda n, p=p: main_out(p, n).start())
    each(1, 32, lambda n: lo_out(n).start())

    vmain[pl.ds(pl.multiple_of(dp * 16, 16), 16), :] = u[0:16, :]
    vlo[dp] = ulo[0]
    for t in range(CDEV // 256):
        cols = slice(t * 256, (t + 1) * 256)
        own[:, cols] = dot(order[...], u[:, cols]).astype(BF16)
    save_own = pltpu.make_async_copy(own, own_hbm, own_sem)
    save_own.start()

    saves = []
    for p, (lo, hi) in enumerate(OUT_PARTS):
        part_cols = pl.ds(lo, hi - lo)

        def landed(n, p=p, part_cols=part_cols):
            at = vmain.at[pl.ds(pl.multiple_of(ahead(n) * 16, 16), 16), part_cols]
            pltpu.make_async_copy(at, at, ro.at[p, n]).wait()
        each(1, 32, landed)
        for at in range(lo, hi, 256):
            cols = slice(at, at + 256)
            up[:MAIN, cols] = dot(back_m[...], vmain[:, cols]).astype(BF16)
        cp = pltpu.make_async_copy(up.at[pl.ds(0, MAIN), part_cols], up_hbm.at[pl.ds(0, MAIN), part_cols], up_sem.at[p])
        cp.start()
        saves.append(cp)
    each(1, 32, lambda n: arrive(vlo.at[ahead(n)], rlo, n))
    vl[...] = vlo[...].astype(F32).reshape(64, CDEV).astype(BF16)
    up[MAIN:, :] = dot(back_l[...], vl[...]).astype(BF16)
    cp = pltpu.make_async_copy(up.at[pl.ds(MAIN, 64)], up_hbm.at[pl.ds(MAIN, 64)], up_sem.at[len(OUT_PARTS)])
    cp.start()
    saves.append(cp)

    for j in range(1, 8):
        one(j).wait_send()
    for j in range(1, 16):
        two(j).wait_send()
    each(1, 32, lambda n: lo_in(n).wait_send())
    each(EARLY, 32, lambda n: main_in(n).wait_send())
    e1.sent()
    e2.sent()
    for p in range(len(OUT_PARTS)):
        each(1, 32, lambda n, p=p: main_out(p, n).wait_send())
    each(1, 32, lambda n: lo_out(n).wait_send())
    save_nm.wait()
    save_own.wait()
    for cp in saves:
        cp.wait()


def step(owner, cls, g, m):
    D, V = pltpu.SemaphoreType.DMA, pltpu.VMEM
    wide = (ROWS, CDEV)
    square = (ROWS, ROWS)
    return pl.pallas_call(
        kernel,
        out_shape=(jax.ShapeDtypeStruct(wide, F32), jax.ShapeDtypeStruct(wide, BF16), jax.ShapeDtypeStruct(wide, BF16)),
        in_specs=[pl.BlockSpec(memory_space=pltpu.SMEM)] * 2 + [pl.BlockSpec(memory_space=pl.ANY)] * 2,
        out_specs=(pl.BlockSpec(memory_space=pl.ANY),) * 3,
        scratch_shapes=[
            V(wide, F32), V(wide, F32), V(wide, F32), V(wide, BF16),
            V((MAIN, CDEV), BF16), V((MATS, 2, CDEV), BF16), V((MATS, 2, CDEV), BF16), V(wide, BF16),
            V((8, 8, 128), F32), V((16, 8, 128), F32),
            V((MAIN, MAIN), BF16), V((64, 64), BF16), V((MAIN, MAIN), BF16), V((64, 64), BF16), V(square, BF16),
            V((4 * Q_FIRST, 32, 128), F32), V((4 * Q_LAST, 32, 128), F32),
            V((2, Q_FIRST, 32, 128), F32), V((Q_FIRST, 32, 128), F32),
            V((2, Q_LAST, 32, 128), F32), V((Q_LAST, 32, 128), F32),
            V((4 * Q_FIRST, 32, 128), F32), V((4 * Q_LAST, 32, 128), F32),
            V(square, F32), V(square, F32), V((ITERS, ROWS, ROWS), BF16),
            V(wide, BF16), V((MATS, 2, CDEV), BF16), V((MAIN, CDEV), BF16), V((MATS, 2, CDEV), BF16), V((64, CDEV), BF16),
            V(wide, BF16), V(wide, BF16),
            D((2, LOADS)), D, D, D((len(OUT_PARTS) + 1,)),
            D((8,)), D((8,)), D((16,)), D((16,)), D((32,)), D((32,)), D((32,)), D((32,)),
            D((len(OUT_PARTS), 32)), D((len(OUT_PARTS), 32)), D((32,)), D((32,)), D((12,)), D((12,)),
        ],
        compiler_params=pltpu.CompilerParams(collective_id=0, has_side_effects=True, vmem_limit_bytes=VMEM_LIMIT),
    )(owner, cls, g, m)


PIECES = 4


def place_kernel(*refs):
    sems = refs[6]
    copies = []
    for i in range(3):
        for k in range(PIECES):
            rows = pl.ds(k * (ROWS // PIECES), ROWS // PIECES)
            copies.append(pltpu.make_async_copy(refs[i].at[rows], refs[3 + i].at[rows], sems.at[i, k]))
    for cp in copies:
        cp.start()
    for cp in copies:
        cp.wait()


def placed(*arrays):
    return pl.pallas_call(
        place_kernel,
        out_shape=tuple(jax.ShapeDtypeStruct(a.shape, a.dtype) for a in arrays),
        in_specs=[pl.BlockSpec(memory_space=pl.ANY)] * 3,
        out_specs=(pl.BlockSpec(memory_space=pl.ANY),) * 3,
        scratch_shapes=[pltpu.SemaphoreType.DMA((3, PIECES))],
    )(*arrays)


def body(gradient, momentum, owner_table, shape_class):
    g = jnp.transpose(gradient, (1, 0, 2)).reshape(ROWS, CDEV)
    m = jnp.transpose(momentum, (1, 0, 2)).reshape(ROWS, CDEV)
    nm, up, own = placed(*step(owner_table, shape_class, g, m))
    new_moment = jnp.transpose(nm.reshape(RDEV, MATS, CDEV), (1, 0, 2))
    update = jnp.transpose(up.reshape(RDEV, MATS, CDEV), (1, 0, 2))
    return new_moment, update, own[None]


def solution(mesh):
    return jax.shard_map(
        body,
        mesh=mesh,
        in_specs=(P(None, "dp", "expert"), P(None, "dp", "expert"), P(), P()),
        out_specs=(P(None, "dp", "expert"), P(None, "dp", "expert"), P("dp", None, "expert")),
        check_vma=False,
    )
```

```python
import math

import jax
import jax.numpy as jnp
from jax import lax
from jax.experimental import pallas as pl
from jax.experimental.pallas import tpu as pltpu
from jax.sharding import PartitionSpec as P

MESH = pl.DeviceIdType.MESH
F32, BF16 = jnp.float32, jnp.bfloat16
ROWS, COLS, MATS, RDEV, CDEV = 576, 7168, 32, 18, 1792
ROUTER_ROWS = 384
LOADS = 6
MU_RATE, EPSILON = 0.95, 1e-07
COEF_A, COEF_B, COEF_C, ITERS = 3.4445, -4.775, 2.0315, 4
SCALE = 0.2 * math.sqrt(COLS)
VMEM_LIMIT = 44 * 1024 * 1024
MAIN = 512
OUT_PARTS = ((0, 256), (256, 768), (768, CDEV))
WINDOW = 12
PAIRS = ((0, 0), (2, 2), (1, 0), (0, 1), (3, 0), (0, 3), (2, 0), (0, 2),
         (1, 2), (2, 1), (3, 2), (2, 3),
         (1, 1), (3, 3), (1, 3), (3, 1))
SLOTS = tuple((dy, dz, dc) for dy, dz in PAIRS for dc in (0, 1))
GROUPS = (16, 24, 32)
SHORT = 16 * GROUPS[0]
TOPS = (SHORT + 64, 16 * GROUPS[1] + 64, ROWS)
PANELS = tuple(tuple((r, t) for r in range(lo // 64, hi // 64) for t in range(r // 2 + 1))
               for lo, hi in zip((0,) + TOPS, TOPS))
QUARTERS = tuple(-(-2 * len(p) // 4) for p in PANELS)


def dot(a, b):
    return jnp.dot(a, b, preferred_element_type=F32)


def dot_t(a, b):
    return lax.dot_general(a, b, (((1,), (1,)), ((), ())), preferred_element_type=F32)


def one_hot(match):
    return match.astype(F32).astype(BF16)


def halving_places(ex, c):
    near = ex + 1 - 2 * (ex % 2)
    far = 3 - ex
    first = (1 - c) * near + c * far
    second = (1 - c) * far + c * near

    def part(x):
        h = (1 - c) * (((x + 1) // 2) % 2) + c * (x // 2)
        q = (1 - c) * (x // 2) + c * (x % 2)
        return h, q
    return first, second, part


def row_at(n):
    return 16 * n + (64 if n >= GROUPS[0] else 0)


def kernel(owner_s, cls_s, g_hbm, m_hbm, nm_hbm, up_hbm, own_hbm,
           g, m, nm, zs, zmain, zlo, lor, x, ar1, ar2,
           perm_m, perm_l, back_m, back_l, order, *rest):
    sums = [rest[4 * i:4 * i + 4] for i in range(3)]
    (gram, t_ref, left, right, coef, u, ulo, vmain, vlo, vl, up, own,
     in_sem, nm_sem, own_sem, up_sem, s1, r1, s2, r2, sm, rm, sl, rl, so, ro, slo, rlo, xs, xr) = rest[12:]
    dp, ex = lax.axis_index("dp"), lax.axis_index("expert")
    y, z, c = dp // 8, (dp // 2) % 4, dp % 2

    def ahead(n):
        dy, dz, dc = SLOTS[n]
        return (((y + dy) % 4) * 4 + (z + dz) % 4) * 2 + (c + dc) % 2

    def behind(n):
        dy, dz, dc = SLOTS[n]
        return (((y + 4 - dy) % 4) * 4 + (z + 4 - dz) % 4) * 2 + (c + dc) % 2

    per = ROWS // LOADS
    loads = []
    for k in range(LOADS):
        rows = pl.ds(k * per, per)
        for n, (src, dst) in enumerate(((g_hbm, g), (m_hbm, m))):
            cp = pltpu.make_async_copy(src.at[rows], dst.at[rows], in_sem.at[n, k])
            cp.start()
            loads.append(cp)

    barrier = pltpu.get_barrier_semaphore()

    def greet(j, _):
        to = (((y + j // 8) % 4) * 4 + (z + (j // 2) % 4) % 4) * 2 + (c + j % 2) % 2
        pl.semaphore_signal(barrier, inc=1, device_id=(to, ex), device_id_type=MESH)
        return _
    lax.fori_loop(1, 32, greet, 0)

    def greet_x(j, _):
        zz, xx = (z + j % 4) % 4, (ex + j // 4) % 4
        pl.semaphore_signal(barrier, inc=1, device_id=((y * 4 + zz) * 2 + c, xx), device_id_type=MESH)
        return _
    lax.fori_loop(4, 16, greet_x, 0)

    lane = lax.broadcasted_iota(jnp.int32, (8, ROWS), 1)
    mat = lax.broadcasted_iota(jnp.int32, (MATS, 128), 0)
    owner_row = jnp.zeros((8, ROWS), jnp.int32)
    cls = jnp.zeros((MATS, 128), F32)
    for i in range(MATS):
        owner_row = jnp.where(lane % MATS == i, owner_s[i], owner_row)
        cls = jnp.where(mat == i, cls_s[i].astype(F32), cls)
    wanted = (owner_row * RDEV + lane // MATS)[0:1]
    o = lax.broadcasted_iota(jnp.int32, (32, MAIN), 0)
    key = (o // 16) * RDEV + o % 16
    for k in range(16):
        perm_m[32 * k:32 * (k + 1), :] = one_hot(key + 2 * RDEV * k == wanted[:, :MAIN])
    o = lax.broadcasted_iota(jnp.int32, (64, 64), 0)
    perm_l[...] = one_hot((o // 2) * RDEV + 16 + o % 2 == wanted[:, MAIN:])

    def live_at(r):
        return jnp.where(dp * RDEV + r < ROUTER_ROWS, 1.0, 1.0 - cls)

    def rows_of(r):
        return pl.ds(pl.multiple_of(r * MATS, MATS), MATS)

    def stats(r, acc):
        live = live_at(r)
        gg, gm, mm = acc
        for t in range(CDEV // 128):
            cols = slice(t * 128, (t + 1) * 128)
            gv = g[rows_of(r), cols] * live
            mv = m[rows_of(r), cols] * (live * (MU_RATE * MU_RATE))
            gg, gm, mm = gg + gv * gv, gm + gv * mv, mm + mv * mv
        return gg, gm, mm

    acc = (jnp.zeros((MATS, 128), F32),) * 3
    for k in range(LOADS):
        loads[2 * k].wait()
        loads[2 * k + 1].wait()
        acc = lax.fori_loop(k * (RDEV // LOADS), (k + 1) * (RDEV // LOADS), stats, acc)
    tots = [jnp.sum(a, axis=1, keepdims=True) for a in acc]
    col = lax.broadcasted_iota(jnp.int32, (MATS, 128), 1)
    mine = jnp.where(col == 0, tots[0], jnp.where(col == 1, tots[1], jnp.where(col == 2, tots[2], 0.0)))
    mine = jnp.concatenate([mine, jnp.zeros((128 - MATS, 128), F32)], axis=0).T[:8]

    pl.semaphore_wait(barrier, 31 + 12)

    i1, i2 = y * 2 + c, ex * 4 + z
    ar1[i1] = mine

    def got(buf, slot, sem):
        return pltpu.make_async_copy(buf.at[slot], buf.at[slot], sem.at[slot])

    def one_of(j):
        return (y + j // 2) % 4, (c + j % 2) % 2

    def one(j):
        yy, cc = one_of(j)
        return pltpu.make_async_remote_copy(
            src_ref=ar1.at[i1], dst_ref=ar1.at[i1], send_sem=s1.at[j], recv_sem=r1.at[i1],
            device_id=((yy * 4 + z) * 2 + cc, ex), device_id_type=MESH)

    def two_of(j):
        return (z + j % 4) % 4, (ex + j // 4) % 4

    def two(j):
        zz, xx = two_of(j)
        return pltpu.make_async_remote_copy(
            src_ref=ar2.at[i2], dst_ref=ar2.at[i2], send_sem=s2.at[j], recv_sem=r2.at[i2],
            device_id=((y * 4 + zz) * 2 + c, xx), device_id_type=MESH)

    for j in range(1, 8):
        one(j).start()
    for j in range(1, 8):
        yy, cc = one_of(j)
        got(ar1, yy * 2 + cc, r1).wait()
    ar2[i2] = jnp.sum(ar1[...], axis=0)
    for j in range(1, 16):
        two(j).start()
    for j in range(1, 16):
        zz, xx = two_of(j)
        got(ar2, xx * 4 + zz, r2).wait()
    tot = jnp.concatenate([jnp.sum(ar2[...], axis=0), jnp.zeros((120, 128), F32)], axis=0).T[:MATS]
    gg, gm, mm = tot[:, 0:1], tot[:, 1:2], tot[:, 2:3]
    total = jnp.sum(gg, axis=0, keepdims=True)
    clip = jnp.minimum(1.0, jnp.sqrt(float(MATS * ROWS * COLS) / total))
    rate = (1.0 + MU_RATE) * clip
    sq = jnp.where(clip > 0.0, rate * rate * gg + 2.0 * rate * gm, 0.0) + mm
    norm = jnp.sqrt(jnp.maximum(sq, 0.0))
    inv = jnp.broadcast_to(1.0 / (norm + EPSILON), (MATS, 128))
    clip = jnp.broadcast_to(clip, (MATS, 128))

    def blend(r, _):
        live = live_at(r)
        lc = live * clip
        lm = live * MU_RATE
        for t in range(CDEV // 128):
            cols = slice(t * 128, (t + 1) * 128)
            gv = g[rows_of(r), cols] * lc
            nv = m[rows_of(r), cols] * lm + gv
            nm[rows_of(r), cols] = nv
            zs[rows_of(r), cols] = ((gv + MU_RATE * nv) * inv).astype(BF16)
        return _
    lax.fori_loop(0, RDEV, blend, 0)
    for t in range(CDEV // 256):
        cols = slice(t * 256, (t + 1) * 256)
        zmain[:, cols] = dot(perm_m[...], zs[:MAIN, cols]).astype(BF16)
        zlo[:, :, cols] = dot(perm_l[...], zs[MAIN:, cols]).reshape(MATS, 2, 256).astype(BF16)

    def block(ref, i):
        return ref.at[pl.ds(pl.multiple_of(i * 16, 16), 16)]

    def slot(ref, n):
        return ref.at[pl.ds(row_at(n), 16)]

    def main_in(n):
        to = ahead(n)
        return pltpu.make_async_remote_copy(
            src_ref=block(zmain, to), dst_ref=slot(x, n), send_sem=sm.at[n], recv_sem=rm.at[n],
            device_id=(to, ex), device_id_type=MESH)

    def lo_in(n):
        to = ahead(n)
        return pltpu.make_async_remote_copy(
            src_ref=zlo.at[to], dst_ref=lor.at[n], send_sem=sl.at[n], recv_sem=rl.at[n],
            device_id=(to, ex), device_id_type=MESH)

    def each(lo, hi, act):
        for n in range(lo, hi):
            act(n)

    def go(n):
        if n > WINDOW:
            main_in(n - WINDOW).wait_send()
        main_in(n).start()

    each(1, 32, lambda n: lo_in(n).start())
    each(1, WINDOW + 1, go)
    save_nm = pltpu.make_async_copy(nm, nm_hbm, nm_sem)
    save_nm.start()
    x[0:16, :] = zmain[pl.ds(pl.multiple_of(dp * 16, 16), 16), :]
    lor[0] = zlo[dp]

    owner_col = jnp.zeros((MATS, MAIN), jnp.int32)
    mats = lax.broadcasted_iota(jnp.int32, (MATS, MAIN), 0)
    for i in range(MATS):
        owner_col = jnp.where(mats == i, owner_s[i], owner_col)
    owner_col = owner_col * RDEV
    key = ((lane // 16) * RDEV + lane % 16)[0:1, :MAIN]
    for r in range(16):
        back_m[MATS * r:MATS * (r + 1), :] = one_hot(owner_col + r == key)
    key = ((lane // 2) * RDEV + 16 + lane % 2)[0:1, :64]
    for r in range(2):
        back_l[MATS * r:MATS * (r + 1), :] = one_hot(owner_col[:, :64] + (16 + r) == key)
    short = (lane >= SHORT) & (lane < SHORT + 64)
    n = jnp.where(short, (lane - SHORT) // 2, jnp.where(lane < SHORT, lane // 16, lane // 16 - 4))
    source = jnp.zeros((8, ROWS), jnp.int32)
    for k in range(32):
        source = jnp.where(n == k, behind(k), source)
    key = (source * RDEV + jnp.where(short, 16 + lane % 2, lane % 16))[0:1]
    for k in range(RDEV):
        rows = lax.broadcasted_iota(jnp.int32, (MATS, ROWS), 0) + MATS * k
        order[MATS * k:MATS * (k + 1), :] = one_hot(rows == key)

    each(WINDOW + 1, GROUPS[0] + WINDOW, go)

    def arrive(ref_at, sem, n):
        pltpu.make_async_copy(ref_at, ref_at, sem.at[n]).wait()

    each(1, GROUPS[0], lambda n: arrive(slot(x, n), rm, n))
    each(1, 32, lambda n: arrive(lor.at[n], rl, n))
    x[SHORT:SHORT + 64, :] = lor[...].astype(F32).reshape(64, CDEV).astype(BF16)

    def put(part, n, piece):
        if piece.shape[1] < 128:
            piece = jnp.concatenate([piece, jnp.zeros((64, 128 - piece.shape[1]), F32)], axis=1)
        part[2 * n] = piece[:32]
        part[2 * n + 1] = piece[32:]

    def terms(i, part):
        low, top = (0,) + TOPS[:2], TOPS[i]
        low = low[i]
        for lo, hi in (((0, 256), (256, top)) if i == 0 else ((0, top),)):
            lo_row = max(low, lo)
            gb = dot_t(x[lo_row:top, :], x[lo:hi, :])
            for n, (r, t) in enumerate(PANELS[i]):
                if lo <= 128 * t < hi:
                    put(part, n, gb[64 * r - lo_row:64 * r - lo_row + 64, 128 * t - lo:min(128 * t + 128, hi) - lo])
        for n in range(2 * len(PANELS[i]), 4 * QUARTERS[i]):
            part[n] = jnp.zeros((32, 128), F32)

    first, second, part_of = halving_places(ex, c)
    h, q = part_of(ex)
    h1, q1 = part_of(first)

    class Sum:
        def __init__(self, part, got_a, got_b, full, size, base):
            self.part, self.got_a, self.got_b, self.full, self.size, self.base = part, got_a, got_b, full, size, base

        def at(self, hh, qq):
            return pl.ds((2 * hh + qq) * self.size, self.size)

        def move(self, src, dst, n, to):
            return pltpu.make_async_remote_copy(
                src_ref=src, dst_ref=dst, send_sem=xs.at[self.base + n], recv_sem=xr.at[self.base + n],
                device_id=(dp, to), device_id_type=MESH)

        def halves(self):
            self.a1 = self.move(self.part.at[self.at(h1, 1 - q1)], self.got_a.at[0], 0, first)
            self.a2 = self.move(self.part.at[self.at(h1, q1)], self.got_a.at[1], 1, first)
            self.a1.start()
            self.a2.start()

        def quarters(self):
            self.a1.wait_recv()
            pass_on = self.at(h, 1 - q)
            self.part[pass_on] = self.part[pass_on] + self.got_a[0]
            self.b = self.move(self.part.at[pass_on], self.got_b, 2, second)
            self.b.start()

        def finish(self):
            self.a2.wait_recv()
            self.b.wait_recv()
            keep = self.at(h, q)
            self.full[keep] = self.part[keep] + self.got_a[1] + self.got_b[...]
            self.c1 = self.move(self.full.at[keep], self.full.at[keep], 3, second)
            self.c2 = self.move(self.full.at[keep], self.full.at[keep], 4, first)
            self.c1.start()
            self.c2.start()

        def forward(self):
            self.c1.wait_recv()
            other = self.at(h, 1 - q)
            self.c3 = self.move(self.full.at[other], self.full.at[other], 5, first)
            self.c3.start()

        def done(self):
            self.c2.wait_recv()
            self.c3.wait_recv()

        def sent(self):
            for cp in (self.a1, self.a2, self.b, self.c1, self.c2, self.c3):
                cp.wait_send()

    def lay_out(i, full):
        for n, (r, t) in enumerate(PANELS[i]):
            w = min(128, TOPS[i] - 128 * t)
            piece = jnp.concatenate([full[2 * n], full[2 * n + 1]], axis=0)
            gram[64 * r:64 * r + 64, 128 * t:128 * t + w] = piece[:, :w]
            if 128 * t + w <= 64 * r:
                gram[128 * t:128 * t + w, 64 * r:64 * r + 64] = piece.T[:w]
            elif 128 * t < 64 * r:
                gram[128 * t:64 * r, 64 * r:64 * r + 64] = piece.T[:64 * r - 128 * t]

    e1, e2, e3 = (Sum(*sums[i], QUARTERS[i], 6 * i) for i in range(3))
    terms(0, e1.part)
    e1.halves()
    each(GROUPS[0] + WINDOW, 32, go)
    e1.quarters()
    each(GROUPS[0], GROUPS[1], lambda n: arrive(slot(x, n), rm, n))
    terms(1, e2.part)
    e2.halves()
    e1.finish()
    e2.quarters()
    e1.forward()
    each(GROUPS[1], 32, lambda n: arrive(slot(x, n), rm, n))
    terms(2, e3.part)
    e3.halves()
    e2.finish()
    e1.done()
    lay_out(0, e1.full)
    e2.forward()
    e3.quarters()
    e2.done()
    lay_out(1, e2.full)
    e3.finish()
    e3.forward()
    e3.done()
    lay_out(2, e3.full)

    left[:, ROWS:640] = jnp.zeros((ROWS, 64), BF16)
    left[:, 640 + ROWS:] = jnp.zeros((ROWS, 64), BF16)
    right[ROWS:640, :] = jnp.zeros((64, ROWS), BF16)
    right[640 + ROWS:, :] = jnp.zeros((64, ROWS), BF16)
    for k in range(ITERS):
        a16 = gram[...].astype(BF16)
        b16 = (COEF_B * a16.astype(F32) + COEF_C * dot(a16, a16)).astype(BF16)
        coef[k] = b16
        if k + 1 < ITERS:
            left[:, :ROWS] = a16
            left[:, 640:640 + ROWS] = (gram[...] - a16.astype(F32)).astype(BF16)
            right[:ROWS, :] = b16
            right[640:640 + ROWS, :] = b16
            t_ref[...] = COEF_A * gram[...] + dot(left[...], right[...])
            left[:, :ROWS] = b16
            left[:, 640:640 + ROWS] = b16
            t16 = t_ref[...].astype(BF16)
            right[:ROWS, :] = t16
            right[640:640 + ROWS, :] = (t_ref[...] - t16.astype(F32)).astype(BF16)
            gram[...] = COEF_A * t_ref[...] + dot(left[...], right[...])

    def main_out(p, n):
        to = behind(n)
        cols = pl.ds(OUT_PARTS[p][0], OUT_PARTS[p][1] - OUT_PARTS[p][0])
        return pltpu.make_async_remote_copy(
            src_ref=u.at[pl.ds(row_at(n), 16), cols],
            dst_ref=vmain.at[pl.ds(pl.multiple_of(dp * 16, 16), 16), cols],
            send_sem=so.at[p, n], recv_sem=ro.at[p, n], device_id=(to, ex), device_id_type=MESH)

    def lo_out(n):
        to = behind(n)
        return pltpu.make_async_remote_copy(
            src_ref=ulo.at[n], dst_ref=vlo.at[dp], send_sem=slo.at[n], recv_sem=rlo.at[n],
            device_id=(to, ex), device_id_type=MESH)

    for p, (lo, hi) in enumerate(OUT_PARTS):
        for at in range(lo, hi, 512):
            cols = slice(at, min(at + 512, hi))
            cur = x[:, cols]
            for k in range(ITERS):
                out = COEF_A * cur.astype(F32) + dot(coef[k], cur)
                if k + 1 < ITERS:
                    cur = out.astype(BF16)
            res = (SCALE * out).astype(BF16)
            u[:, cols] = res
            ulo[:, :, cols] = res[SHORT:SHORT + 64].astype(F32).reshape(MATS, 2, cols.stop - at).astype(BF16)
        each(1, 32, lambda n, p=p: main_out(p, n).start())
    each(1, 32, lambda n: lo_out(n).start())

    vmain[pl.ds(pl.multiple_of(dp * 16, 16), 16), :] = u[0:16, :]
    vlo[dp] = ulo[0]
    for t in range(CDEV // 256):
        cols = slice(t * 256, (t + 1) * 256)
        own[:, cols] = dot(order[...], u[:, cols]).astype(BF16)
    save_own = pltpu.make_async_copy(own, own_hbm, own_sem)
    save_own.start()

    saves = []
    for p, (lo, hi) in enumerate(OUT_PARTS):
        part_cols = pl.ds(lo, hi - lo)

        def landed(n, p=p, part_cols=part_cols):
            at = vmain.at[pl.ds(pl.multiple_of(ahead(n) * 16, 16), 16), part_cols]
            pltpu.make_async_copy(at, at, ro.at[p, n]).wait()
        each(1, 32, landed)
        for at in range(lo, hi, 256):
            cols = slice(at, at + 256)
            up[:MAIN, cols] = dot(back_m[...], vmain[:, cols]).astype(BF16)
        cp = pltpu.make_async_copy(up.at[pl.ds(0, MAIN), part_cols], up_hbm.at[pl.ds(0, MAIN), part_cols], up_sem.at[p])
        cp.start()
        saves.append(cp)
    each(1, 32, lambda n: arrive(vlo.at[ahead(n)], rlo, n))
    vl[...] = vlo[...].astype(F32).reshape(64, CDEV).astype(BF16)
    up[MAIN:, :] = dot(back_l[...], vl[...]).astype(BF16)
    cp = pltpu.make_async_copy(up.at[pl.ds(MAIN, 64)], up_hbm.at[pl.ds(MAIN, 64)], up_sem.at[len(OUT_PARTS)])
    cp.start()
    saves.append(cp)

    for j in range(1, 8):
        one(j).wait_send()
    for j in range(1, 16):
        two(j).wait_send()
    each(1, 32, lambda n: lo_in(n).wait_send())
    each(32 - WINDOW, 32, lambda n: main_in(n).wait_send())
    for e in (e1, e2, e3):
        e.sent()
    for p in range(len(OUT_PARTS)):
        each(1, 32, lambda n, p=p: main_out(p, n).wait_send())
    each(1, 32, lambda n: lo_out(n).wait_send())
    save_nm.wait()
    save_own.wait()
    for cp in saves:
        cp.wait()


def step(owner, cls, g, m):
    D, V = pltpu.SemaphoreType.DMA, pltpu.VMEM
    wide = (ROWS, CDEV)
    square = (ROWS, ROWS)
    return pl.pallas_call(
        kernel,
        out_shape=(jax.ShapeDtypeStruct(wide, F32), jax.ShapeDtypeStruct(wide, BF16), jax.ShapeDtypeStruct(wide, BF16)),
        in_specs=[pl.BlockSpec(memory_space=pltpu.SMEM)] * 2 + [pl.BlockSpec(memory_space=pl.ANY)] * 2,
        out_specs=(pl.BlockSpec(memory_space=pl.ANY),) * 3,
        scratch_shapes=[
            V(wide, F32), V(wide, F32), V(wide, F32), V(wide, BF16),
            V((MAIN, CDEV), BF16), V((MATS, 2, CDEV), BF16), V((MATS, 2, CDEV), BF16), V(wide, BF16),
            V((8, 8, 128), F32), V((16, 8, 128), F32),
            V((MAIN, MAIN), BF16), V((64, 64), BF16), V((MAIN, MAIN), BF16), V((64, 64), BF16), V(square, BF16),
            *[V((k * q, 32, 128), F32) if k else V((2, q, 32, 128), F32) for q in QUARTERS for k in (4, 0, 1, 4)],
            V(square, F32), V(square, F32), V((ROWS, 1280), BF16), V((1280, ROWS), BF16), V((ITERS, ROWS, ROWS), BF16),
            V(wide, BF16), V((MATS, 2, CDEV), BF16), V((MAIN, CDEV), BF16), V((MATS, 2, CDEV), BF16), V((64, CDEV), BF16),
            V(wide, BF16), V(wide, BF16),
            D((2, LOADS)), D, D, D((len(OUT_PARTS) + 1,)),
            D((8,)), D((8,)), D((16,)), D((16,)), D((32,)), D((32,)), D((32,)), D((32,)),
            D((len(OUT_PARTS), 32)), D((len(OUT_PARTS), 32)), D((32,)), D((32,)), D((18,)), D((18,)),
        ],
        compiler_params=pltpu.CompilerParams(collective_id=0, has_side_effects=True, vmem_limit_bytes=VMEM_LIMIT),
    )(owner, cls, g, m)


PIECES = 4


def place_kernel(*refs):
    copies = []
    for i in range(3):
        for k in range(PIECES):
            rows = pl.ds(k * (ROWS // PIECES), ROWS // PIECES)
            copies.append(pltpu.make_async_copy(refs[i].at[rows], refs[3 + i].at[rows], refs[6].at[i, k]))
    for cp in copies:
        cp.start()
    for cp in copies:
        cp.wait()


def placed(*arrays):
    return pl.pallas_call(
        place_kernel,
        out_shape=tuple(jax.ShapeDtypeStruct(a.shape, a.dtype) for a in arrays),
        in_specs=[pl.BlockSpec(memory_space=pl.ANY)] * 3,
        out_specs=(pl.BlockSpec(memory_space=pl.ANY),) * 3,
        scratch_shapes=[pltpu.SemaphoreType.DMA((3, PIECES))],
    )(*arrays)


def body(gradient, momentum, owner_table, shape_class):
    g = jnp.transpose(gradient, (1, 0, 2)).reshape(ROWS, CDEV)
    m = jnp.transpose(momentum, (1, 0, 2)).reshape(ROWS, CDEV)
    nm, up, own = placed(*step(owner_table, shape_class, g, m))
    new_moment = jnp.transpose(nm.reshape(RDEV, MATS, CDEV), (1, 0, 2))
    update = jnp.transpose(up.reshape(RDEV, MATS, CDEV), (1, 0, 2))
    return new_moment, update, own[None]


def solution(mesh):
    return jax.shard_map(
        body,
        mesh=mesh,
        in_specs=(P(None, "dp", "expert"), P(None, "dp", "expert"), P(), P()),
        out_specs=(P(None, "dp", "expert"), P(None, "dp", "expert"), P("dp", None, "expert")),
        check_vma=False,
    )
```

```python
import math

import jax
import jax.numpy as jnp
from jax import lax
from jax.experimental import pallas as pl
from jax.experimental.pallas import tpu as pltpu
from jax.sharding import PartitionSpec as P

MESH = pl.DeviceIdType.MESH
F32, BF16 = jnp.float32, jnp.bfloat16
ROWS, COLS, MATS, RDEV, CDEV = 576, 7168, 32, 18, 1792
ROUTER_ROWS = 384
LOADS = 6
MU_RATE, EPSILON = 0.95, 1e-07
COEF_A, COEF_B, COEF_C, ITERS = 3.4445, -4.775, 2.0315, 4
SCALE = 0.2 * math.sqrt(COLS)
VMEM_LIMIT = 44 * 1024 * 1024
MAIN = 512
OUT_PARTS = ((0, 256), (256, 768), (768, CDEV))
WINDOW = 12
GROUPS = (16, 24, 32)
SHORT = 16 * GROUPS[0]
TOPS = (SHORT + 64, 16 * GROUPS[1] + 64, ROWS)
PANELS = tuple(tuple((r, t) for r in range(lo // 64, hi // 64) for t in range(r // 2 + 1))
               for lo, hi in zip((0,) + TOPS, TOPS))
QUARTERS = tuple(-(-2 * len(p) // 4) for p in PANELS)


def dot(a, b):
    return jnp.dot(a, b, preferred_element_type=F32)


def dot_t(a, b):
    return lax.dot_general(a, b, (((1,), (1,)), ((), ())), preferred_element_type=F32)


def away(n, group):
    k, s = lax.rem(lax.div(n, 4), 4), lax.rem(lax.div(n, 2), 2)
    if group == 0:
        both = 2 * lax.div(3 - k, 3) * s
        dy, dz = k * (1 - s) + both, k * s + both
    elif group == 1:
        odd = 1 + 2 * lax.rem(k, 2)
        dy, dz = odd * (1 - s) + 2 * s, 2 * (1 - s) + odd * s
    else:
        dy, dz = 1 + 2 * s, 1 + 2 * lax.rem(s + k, 2)
    return dy, dz, lax.rem(n, 2)


def one_hot(match):
    return match.astype(F32).astype(BF16)


def row_at(n, group):
    return pl.multiple_of(16 * n + (64 if group else 0), 16)


def kernel(owner_hbm, cls_hbm, g_hbm, m_hbm, nm_hbm, up_hbm, own_hbm,
           g, m, nm, zs, zmain, zlo, lor, x, ar1, ar2,
           perm_m, perm_l, back_m, back_l, order, owner_s, cls_s, *rest):
    sums = [rest[3 * i:3 * i + 3] for i in range(3)]
    (gram, t_ref, left, right, coef, u, ulo, vmain, vlo, vl, up, own,
     in_sem, nm_sem, own_sem, up_sem, s1, r1, s2, r2, sm, rm, sl, rl, so, ro, slo, rlo, xs, xr) = rest[9:]
    dp, ex = lax.axis_index("dp"), lax.axis_index("expert")
    y, z, c = dp // 8, (dp // 2) % 4, dp % 2

    def ahead(n, group):
        dy, dz, dc = away(n, group)
        return lax.rem(y + dy, 4) * 8 + lax.rem(z + dz, 4) * 2 + lax.rem(c + dc, 2)

    def behind(n, group):
        dy, dz, dc = away(n, group)
        return lax.rem(y + 4 - dy, 4) * 8 + lax.rem(z + 4 - dz, 4) * 2 + lax.rem(c + dc, 2)

    def each(lo, hi, act):
        for group, (first, end) in enumerate(zip((0,) + GROUPS, GROUPS)):
            if max(lo, first) < min(hi, end):
                def step(n, _, group=group):
                    act(n, group)
                    return _
                lax.fori_loop(max(lo, first), min(hi, end), step, 0)

    per = ROWS // LOADS
    loads = []
    for k in range(LOADS):
        rows = pl.ds(k * per, per)
        for n, (src, dst) in enumerate(((g_hbm, g), (m_hbm, m))):
            cp = pltpu.make_async_copy(src.at[rows], dst.at[rows], in_sem.at[n, k])
            cp.start()
            loads.append(cp)

    tables = [pltpu.make_async_copy(src, dst, up_sem.at[i]) for i, (src, dst) in enumerate(((owner_hbm, owner_s), (cls_hbm, cls_s)))]
    for cp in tables:
        cp.start()
    barrier = pltpu.get_barrier_semaphore()

    each(1, 32, lambda n, group: pl.semaphore_signal(
        barrier, inc=1, device_id=(ahead(n, group), ex), device_id_type=MESH))

    def greet_x(j, _):
        zz, xx = (z + j % 4) % 4, (ex + j // 4) % 4
        pl.semaphore_signal(barrier, inc=1, device_id=((y * 4 + zz) * 2 + c, xx), device_id_type=MESH)
        return _
    lax.fori_loop(4, 16, greet_x, 0)

    for cp in tables:
        cp.wait()

    lane = lax.broadcasted_iota(jnp.int32, (8, ROWS), 1)
    mat = lax.broadcasted_iota(jnp.int32, (MATS, 128), 0)
    owner_row = jnp.zeros((8, ROWS), jnp.int32)
    cls = jnp.zeros((MATS, 128), F32)
    for i in range(MATS):
        owner_row = jnp.where(lane % MATS == i, owner_s[i], owner_row)
        cls = jnp.where(mat == i, cls_s[i].astype(F32), cls)
    wanted = (owner_row * RDEV + lane // MATS)[0:1]
    o = lax.broadcasted_iota(jnp.int32, (32, MAIN), 0)
    key = (o // 16) * RDEV + o % 16
    for k in range(16):
        perm_m[32 * k:32 * (k + 1), :] = one_hot(key + 2 * RDEV * k == wanted[:, :MAIN])
    o = lax.broadcasted_iota(jnp.int32, (64, 64), 0)
    perm_l[...] = one_hot((o // 2) * RDEV + 16 + o % 2 == wanted[:, MAIN:])

    def live_at(r):
        return jnp.where(dp * RDEV + r < ROUTER_ROWS, 1.0, 1.0 - cls)

    def rows_of(r):
        return pl.ds(pl.multiple_of(r * MATS, MATS), MATS)

    def stats(r, acc):
        live = live_at(r)
        gg, gm, mm = acc
        for t in range(CDEV // 128):
            cols = slice(t * 128, (t + 1) * 128)
            gv = g[rows_of(r), cols] * live
            mv = m[rows_of(r), cols] * (live * (MU_RATE * MU_RATE))
            gg, gm, mm = gg + gv * gv, gm + gv * mv, mm + mv * mv
        return gg, gm, mm

    acc = (jnp.zeros((MATS, 128), F32),) * 3
    for k in range(LOADS):
        loads[2 * k].wait()
        loads[2 * k + 1].wait()
        acc = lax.fori_loop(k * (RDEV // LOADS), (k + 1) * (RDEV // LOADS), stats, acc)
    tots = [jnp.sum(a, axis=1, keepdims=True) for a in acc]
    col = lax.broadcasted_iota(jnp.int32, (MATS, 128), 1)
    mine = jnp.where(col == 0, tots[0], jnp.where(col == 1, tots[1], jnp.where(col == 2, tots[2], 0.0)))
    mine = jnp.concatenate([mine, jnp.zeros((128 - MATS, 128), F32)], axis=0).T[:8]

    pl.semaphore_wait(barrier, 31 + 12)

    i1, i2 = y * 2 + c, ex * 4 + z
    ar1[i1] = mine

    def got(buf, slot, sem):
        return pltpu.make_async_copy(buf.at[slot], buf.at[slot], sem.at[slot])

    def one_of(j):
        return (y + j // 2) % 4, (c + j % 2) % 2

    def one(j):
        yy, cc = one_of(j)
        return pltpu.make_async_remote_copy(
            src_ref=ar1.at[i1], dst_ref=ar1.at[i1], send_sem=s1.at[j], recv_sem=r1.at[i1],
            device_id=((yy * 4 + z) * 2 + cc, ex), device_id_type=MESH)

    def two_of(j):
        return (z + j % 4) % 4, (ex + j // 4) % 4

    def two(j):
        zz, xx = two_of(j)
        return pltpu.make_async_remote_copy(
            src_ref=ar2.at[i2], dst_ref=ar2.at[i2], send_sem=s2.at[j], recv_sem=r2.at[i2],
            device_id=((y * 4 + zz) * 2 + c, xx), device_id_type=MESH)

    for j in range(1, 8):
        one(j).start()
    for j in range(1, 8):
        yy, cc = one_of(j)
        got(ar1, yy * 2 + cc, r1).wait()
    ar2[i2] = jnp.sum(ar1[...], axis=0)
    for j in range(1, 16):
        two(j).start()
    for j in range(1, 16):
        zz, xx = two_of(j)
        got(ar2, xx * 4 + zz, r2).wait()
    tot = jnp.concatenate([jnp.sum(ar2[...], axis=0), jnp.zeros((120, 128), F32)], axis=0).T[:MATS]
    gg, gm, mm = tot[:, 0:1], tot[:, 1:2], tot[:, 2:3]
    total = jnp.sum(gg, axis=0, keepdims=True)
    clip = jnp.minimum(1.0, jnp.sqrt(float(MATS * ROWS * COLS) / total))
    rate = (1.0 + MU_RATE) * clip
    sq = jnp.where(clip > 0.0, rate * rate * gg + 2.0 * rate * gm, 0.0) + mm
    bound = rate * rate * gg + mm
    faint = jnp.where((clip > 0.0) & (sq < 1e-4 * bound), 1.0, 0.0)
    sq = jnp.where(faint > 0.0, jnp.maximum(sq, 1e-7 * bound), sq)
    divisor = jnp.sqrt(sq) + EPSILON
    inv = jnp.broadcast_to(1.0 / divisor, (MATS, 128))
    clip = jnp.broadcast_to(clip, (MATS, 128))

    def blend(r, _):
        live = live_at(r)
        lc = live * clip
        lm = live * MU_RATE
        for t in range(CDEV // 128):
            cols = slice(t * 128, (t + 1) * 128)
            gv = g[rows_of(r), cols] * lc
            nv = m[rows_of(r), cols] * lm + gv
            nm[rows_of(r), cols] = nv
            zs[rows_of(r), cols] = ((gv + MU_RATE * nv) * inv).astype(BF16)
        return _
    lax.fori_loop(0, RDEV, blend, 0)
    for t in range(CDEV // 256):
        cols = slice(t * 256, (t + 1) * 256)
        zmain[:, cols] = dot(perm_m[...], zs[:MAIN, cols]).astype(BF16)
        zlo[:, :, cols] = dot(perm_l[...], zs[MAIN:, cols]).reshape(MATS, 2, 256).astype(BF16)

    def block(ref, i):
        return ref.at[pl.ds(pl.multiple_of(i * 16, 16), 16)]

    def slot(ref, n, group):
        return ref.at[pl.ds(row_at(n, group), 16)]

    def main_in(n, group):
        to = ahead(n, group)
        return pltpu.make_async_remote_copy(
            src_ref=block(zmain, to), dst_ref=slot(x, n, group), send_sem=sm.at[n], recv_sem=rm.at[n],
            device_id=(to, ex), device_id_type=MESH)

    def lo_in(n, group):
        to = ahead(n, group)
        return pltpu.make_async_remote_copy(
            src_ref=zlo.at[to], dst_ref=lor.at[n], send_sem=sl.at[n], recv_sem=rl.at[n],
            device_id=(to, ex), device_id_type=MESH)

    def sent(lo, hi):
        each(lo, hi, lambda n, group: main_in(n, group).wait_send())

    each(1, 32, lambda n, group: lo_in(n, group).start())
    each(1, WINDOW + 1, lambda n, group: main_in(n, group).start())
    save_nm = pltpu.make_async_copy(nm, nm_hbm, nm_sem)
    save_nm.start()
    x[0:16, :] = zmain[pl.ds(pl.multiple_of(dp * 16, 16), 16), :]
    lor[0] = zlo[dp]

    owner_col = jnp.zeros((MATS, MAIN), jnp.int32)
    mats = lax.broadcasted_iota(jnp.int32, (MATS, MAIN), 0)
    for i in range(MATS):
        owner_col = jnp.where(mats == i, owner_s[i], owner_col)
    here = owner_col[:, :1] == dp
    divisor = jnp.sum(jnp.where(here, divisor, 0.0), axis=0, keepdims=True)
    faint = jnp.sum(jnp.where(here, faint, 0.0), axis=0, keepdims=True)
    owner_col = owner_col * RDEV
    key = ((lane // 16) * RDEV + lane % 16)[0:1, :MAIN]
    for r in range(16):
        back_m[MATS * r:MATS * (r + 1), :] = one_hot(owner_col + r == key)
    key = ((lane // 2) * RDEV + 16 + lane % 2)[0:1, :64]
    for r in range(2):
        back_l[MATS * r:MATS * (r + 1), :] = one_hot(owner_col[:, :64] + (16 + r) == key)
    short = (lane >= SHORT) & (lane < SHORT + 64)
    n = jnp.where(short, (lane - SHORT) // 2, jnp.where(lane < SHORT, lane // 16, lane // 16 - 4))
    source = jnp.where(n < GROUPS[0], behind(n, 0), jnp.where(n < GROUPS[1], behind(n, 1), behind(n, 2)))
    key = (source * RDEV + jnp.where(short, 16 + lane % 2, lane % 16))[0:1]
    for k in range(RDEV):
        rows = lax.broadcasted_iota(jnp.int32, (MATS, ROWS), 0) + MATS * k
        order[MATS * k:MATS * (k + 1), :] = one_hot(rows == key)

    def go(n, group):
        early = n - WINDOW
        main_in(early, 0).wait_send()
        main_in(n, group).start()
    each(WINDOW + 1, GROUPS[0] + WINDOW, go)

    def arrive(ref_at, sem, n):
        pltpu.make_async_copy(ref_at, ref_at, sem.at[n]).wait()

    each(1, GROUPS[0], lambda n, group: arrive(slot(x, n, group), rm, n))
    each(1, 32, lambda n, group: arrive(lor.at[n], rl, n))
    x[SHORT:SHORT + 64, :] = lor[...].astype(F32).reshape(64, CDEV).astype(BF16)

    def put(part, n, piece):
        if piece.shape[1] < 128:
            piece = jnp.concatenate([piece, jnp.zeros((64, 128 - piece.shape[1]), F32)], axis=1)
        part[2 * n] = piece[:32]
        part[2 * n + 1] = piece[32:]

    def terms(i, part):
        low, top = (0,) + TOPS[:2], TOPS[i]
        low = low[i]
        for lo, hi in (((0, 256), (256, top)) if i == 0 else ((0, top),)):
            lo_row = max(low, lo)
            gb = dot_t(x[lo_row:top, :], x[lo:hi, :])
            for n, (r, t) in enumerate(PANELS[i]):
                if lo <= 128 * t < hi:
                    put(part, n, gb[64 * r - lo_row:64 * r - lo_row + 64, 128 * t - lo:min(128 * t + 128, hi) - lo])
        for n in range(2 * len(PANELS[i]), 4 * QUARTERS[i]):
            part[n] = jnp.zeros((32, 128), F32)

    class Sum:
        def __init__(self, part, got, full, size, base):
            self.part, self.got, self.full, self.size, self.base = part, got, full, size, base

        def at(self, xx):
            return pl.ds(xx * self.size, self.size)

        def move(self, src, dst, n, far):
            return pltpu.make_async_remote_copy(
                src_ref=src, dst_ref=dst, send_sem=xs.at[self.base + n], recv_sem=xr.at[self.base + n],
                device_id=(dp, (ex + far) % 4), device_id_type=MESH)

        def scatter(self):
            self.out = [self.move(self.part.at[self.at((ex + far) % 4)], self.got.at[far - 1], far - 1, far) for far in (2, 1, 3)]
            for cp in self.out:
                cp.start()

        def reduce(self):
            for cp in self.out:
                cp.wait_recv()
            here = self.full.at[self.at(ex)]
            self.full[self.at(ex)] = self.part[self.at(ex)] + self.got[0] + (self.got[1] + self.got[2])
            self.back = [self.move(here, here, 2 + far, far) for far in (2, 1, 3)]
            for cp in self.back:
                cp.start()

        def done(self):
            for cp in self.back:
                cp.wait_recv()

        def sent(self):
            for cp in self.out + self.back:
                cp.wait_send()

    def lay_out(i, full):
        for n, (r, t) in enumerate(PANELS[i]):
            w = min(128, TOPS[i] - 128 * t)
            piece = jnp.concatenate([full[2 * n], full[2 * n + 1]], axis=0)
            gram[64 * r:64 * r + 64, 128 * t:128 * t + w] = piece[:, :w]
            if 128 * t + w <= 64 * r:
                gram[128 * t:128 * t + w, 64 * r:64 * r + 64] = piece.T[:w]
            elif 128 * t < 64 * r:
                gram[128 * t:64 * r, 64 * r:64 * r + 64] = piece.T[:64 * r - 128 * t]

    e1, e2, e3 = (Sum(*sums[i], QUARTERS[i], 6 * i) for i in range(3))
    terms(0, e1.part)
    e1.scatter()

    def rest_go(n, group):
        main_in(n - WINDOW, 1).wait_send()
        main_in(n, group).start()
    each(GROUPS[0] + WINDOW, 32, rest_go)
    e1.reduce()
    each(GROUPS[0], GROUPS[1], lambda n, group: arrive(slot(x, n, group), rm, n))
    terms(1, e2.part)
    e2.scatter()
    e1.done()
    lay_out(0, e1.full)
    e2.reduce()
    each(GROUPS[1], 32, lambda n, group: arrive(slot(x, n, group), rm, n))
    terms(2, e3.part)
    e3.scatter()
    e2.done()
    lay_out(1, e2.full)
    e3.reduce()
    e3.done()
    lay_out(2, e3.full)

    def symmetric(out, a, b, more=None):
        head = dot(a, b[:, :MAIN])
        corner = dot(a[MAIN:, :], b[:, MAIN:])
        if more is not None:
            head = head + COEF_A * more[:, :MAIN]
            corner = corner + COEF_A * more[MAIN:, MAIN:]
        out[:, :MAIN] = head
        out[MAIN:, MAIN:] = corner
        out[:MAIN, MAIN:] = out[MAIN:, :MAIN].T

    diagonal = lax.broadcasted_iota(jnp.int32, (64, 64), 0) == lax.broadcasted_iota(jnp.int32, (64, 64), 1)
    trace = jnp.zeros((64, 64), F32)
    for r in range(ROWS // 64):
        trace = trace + jnp.where(diagonal, gram[64 * r:64 * r + 64, 64 * r:64 * r + 64], 0.0)
    trace = jnp.sum(jnp.sum(trace, axis=1, keepdims=True), axis=0, keepdims=True)
    fit = jnp.where(faint > 0.0, divisor / (jnp.sqrt(trace) * divisor + EPSILON), 1.0)
    gram[...] = gram[...] * (fit * fit)

    left[:, ROWS:640] = jnp.zeros((ROWS, 64), BF16)
    left[:, 640 + ROWS:] = jnp.zeros((ROWS, 64), BF16)
    right[ROWS:640, :] = jnp.zeros((64, ROWS), BF16)
    right[640 + ROWS:, :] = jnp.zeros((64, ROWS), BF16)
    for k in range(ITERS):
        a16 = gram[...].astype(BF16)
        left[:, :ROWS] = a16
        symmetric(t_ref, left[:, :ROWS], a16)
        b16 = (COEF_B * a16.astype(F32) + COEF_C * t_ref[...]).astype(BF16)
        coef[k] = b16
        if k + 1 < ITERS:
            left[:, 640:640 + ROWS] = (gram[...] - a16.astype(F32)).astype(BF16)
            right[:ROWS, :] = b16
            right[640:640 + ROWS, :] = b16
            t_ref[...] = COEF_A * gram[...] + dot(left[...], right[...])
            left[:, :ROWS] = b16
            left[:, 640:640 + ROWS] = b16
            t16 = t_ref[...].astype(BF16)
            right[:ROWS, :] = t16
            right[640:640 + ROWS, :] = (t_ref[...] - t16.astype(F32)).astype(BF16)
            symmetric(gram, left[...], right[...], t_ref)

    def main_out(p, n, group):
        to = behind(n, group)
        cols = pl.ds(OUT_PARTS[p][0], OUT_PARTS[p][1] - OUT_PARTS[p][0])
        return pltpu.make_async_remote_copy(
            src_ref=u.at[pl.ds(row_at(n, group), 16), cols],
            dst_ref=vmain.at[pl.ds(pl.multiple_of(dp * 16, 16), 16), cols],
            send_sem=so.at[p, n], recv_sem=ro.at[p, n], device_id=(to, ex), device_id_type=MESH)

    def lo_out(n, group):
        to = behind(n, group)
        return pltpu.make_async_remote_copy(
            src_ref=ulo.at[n], dst_ref=vlo.at[dp], send_sem=slo.at[n], recv_sem=rlo.at[n],
            device_id=(to, ex), device_id_type=MESH)

    for p, (lo, hi) in enumerate(OUT_PARTS):
        for at in range(lo, hi, 512):
            cols = slice(at, min(at + 512, hi))
            cur = x[:, cols]
            for k in range(ITERS):
                out = COEF_A * cur.astype(F32) + dot(coef[k], cur)
                if k == 0:
                    out = out * fit
                if k + 1 < ITERS:
                    cur = out.astype(BF16)
            res = (SCALE * out).astype(BF16)
            u[:, cols] = res
            ulo[:, :, cols] = res[SHORT:SHORT + 64].astype(F32).reshape(MATS, 2, cols.stop - at).astype(BF16)
        each(1, 32, lambda n, group, p=p: main_out(p, n, group).start())
    each(1, 32, lambda n, group: lo_out(n, group).start())

    vmain[pl.ds(pl.multiple_of(dp * 16, 16), 16), :] = u[0:16, :]
    vlo[dp] = ulo[0]
    for t in range(CDEV // 256):
        cols = slice(t * 256, (t + 1) * 256)
        own[:, cols] = dot(order[...], u[:, cols]).astype(BF16)
    save_own = pltpu.make_async_copy(own, own_hbm, own_sem)
    save_own.start()

    saves = []
    for p, (lo, hi) in enumerate(OUT_PARTS):
        part_cols = pl.ds(lo, hi - lo)

        def landed(n, group, p=p, part_cols=part_cols):
            at = vmain.at[pl.ds(pl.multiple_of(ahead(n, group) * 16, 16), 16), part_cols]
            pltpu.make_async_copy(at, at, ro.at[p, n]).wait()
        each(1, 32, landed)
        for at in range(lo, hi, 256):
            cols = slice(at, at + 256)
            up[:MAIN, cols] = dot(back_m[...], vmain[:, cols]).astype(BF16)
        cp = pltpu.make_async_copy(up.at[pl.ds(0, MAIN), part_cols], up_hbm.at[pl.ds(0, MAIN), part_cols], up_sem.at[p])
        cp.start()
        saves.append(cp)
    each(1, 32, lambda n, group: arrive(vlo.at[ahead(n, group)], rlo, n))
    vl[...] = vlo[...].astype(F32).reshape(64, CDEV).astype(BF16)
    up[MAIN:, :] = dot(back_l[...], vl[...]).astype(BF16)
    cp = pltpu.make_async_copy(up.at[pl.ds(MAIN, 64)], up_hbm.at[pl.ds(MAIN, 64)], up_sem.at[len(OUT_PARTS)])
    cp.start()
    saves.append(cp)

    for j in range(1, 8):
        one(j).wait_send()
    for j in range(1, 16):
        two(j).wait_send()
    each(1, 32, lambda n, group: lo_in(n, group).wait_send())
    sent(32 - WINDOW, 32)
    for e in (e1, e2, e3):
        e.sent()
    for p in range(len(OUT_PARTS)):
        each(1, 32, lambda n, group, p=p: main_out(p, n, group).wait_send())
    each(1, 32, lambda n, group: lo_out(n, group).wait_send())
    save_nm.wait()
    save_own.wait()
    for cp in saves:
        cp.wait()


def step(owner, cls, g, m):
    D, V = pltpu.SemaphoreType.DMA, pltpu.VMEM
    wide = (ROWS, CDEV)
    square = (ROWS, ROWS)
    return pl.pallas_call(
        kernel,
        out_shape=(jax.ShapeDtypeStruct(wide, F32), jax.ShapeDtypeStruct(wide, BF16), jax.ShapeDtypeStruct(wide, BF16)),
        in_specs=[pl.BlockSpec(memory_space=pltpu.HBM)] * 4,
        out_specs=(pl.BlockSpec(memory_space=pl.ANY),) * 3,
        scratch_shapes=[
            V(wide, F32), V(wide, F32), V(wide, F32), V(wide, BF16),
            V((MAIN, CDEV), BF16), V((MATS, 2, CDEV), BF16), V((MATS, 2, CDEV), BF16), V(wide, BF16),
            V((8, 8, 128), F32), V((16, 8, 128), F32),
            V((MAIN, MAIN), BF16), V((64, 64), BF16), V((MAIN, MAIN), BF16), V((64, 64), BF16), V(square, BF16),
            pltpu.SMEM((MATS,), jnp.int32), pltpu.SMEM((MATS,), jnp.int32),
            *[V(shape, F32) for q in QUARTERS for shape in ((4 * q, 32, 128), (3, q, 32, 128), (4 * q, 32, 128))],
            V(square, F32), V(square, F32), V((ROWS, 1280), BF16), V((1280, ROWS), BF16), V((ITERS, ROWS, ROWS), BF16),
            V(wide, BF16), V((MATS, 2, CDEV), BF16), V((MAIN, CDEV), BF16), V((MATS, 2, CDEV), BF16), V((64, CDEV), BF16),
            V(wide, BF16), V(wide, BF16),
            D((2, LOADS)), D, D, D((len(OUT_PARTS) + 1,)),
            D((8,)), D((8,)), D((16,)), D((16,)), D((32,)), D((32,)), D((32,)), D((32,)),
            D((len(OUT_PARTS), 32)), D((len(OUT_PARTS), 32)), D((32,)), D((32,)), D((18,)), D((18,)),
        ],
        compiler_params=pltpu.CompilerParams(collective_id=0, has_side_effects=True, vmem_limit_bytes=VMEM_LIMIT),
    )(owner, cls, g, m)


def body(gradient, momentum, owner_table, shape_class):
    g = jnp.transpose(gradient, (1, 0, 2)).reshape(ROWS, CDEV)
    m = jnp.transpose(momentum, (1, 0, 2)).reshape(ROWS, CDEV)
    nm, up, own = step(owner_table, shape_class, g, m)
    new_moment = jnp.transpose(nm.reshape(RDEV, MATS, CDEV), (1, 0, 2))
    update = jnp.transpose(up.reshape(RDEV, MATS, CDEV), (1, 0, 2))
    return new_moment, update, own[None]


def solution(mesh):
    return jax.shard_map(
        body,
        mesh=mesh,
        in_specs=(P(None, "dp", "expert"), P(None, "dp", "expert"), P(), P()),
        out_specs=(P(None, "dp", "expert"), P(None, "dp", "expert"), P("dp", None, "expert")),
        check_vma=False,
    )
```

```python
import math

import jax
import jax.numpy as jnp
from jax import lax
from jax.experimental import pallas as pl
from jax.experimental.pallas import tpu as pltpu
from jax.sharding import PartitionSpec as P

MESH = pl.DeviceIdType.MESH
F32, BF16 = jnp.float32, jnp.bfloat16
ROWS, COLS, MATS, RDEV, CDEV = 576, 7168, 32, 18, 1792
ROUTER_ROWS = 384
LOADS = 6
MU_RATE, EPSILON = 0.95, 1e-07
COEF_A, COEF_B, COEF_C, ITERS = 3.4445, -4.775, 2.0315, 4
SCALE = 0.2 * math.sqrt(COLS)
VMEM_LIMIT = 44 * 1024 * 1024
MAIN = 512
OUT_PARTS = ((0, 256), (256, 768), (768, CDEV))
WINDOW = 12
GROUPS = (16, 24, 32)
SHORT = 16 * GROUPS[0]
TOPS = (SHORT + 64, 16 * GROUPS[1] + 64, ROWS)
PANELS = tuple(tuple((r, t) for r in range(lo // 64, hi // 64) for t in range(r // 2 + 1))
               for lo, hi in zip((0,) + TOPS, TOPS))
QUARTERS = tuple(-(-2 * len(p) // 4) for p in PANELS)


def dot(a, b):
    return jnp.dot(a, b, preferred_element_type=F32)


def dot_t(a, b):
    return lax.dot_general(a, b, (((1,), (1,)), ((), ())), preferred_element_type=F32)


def away(n, group):
    k, s = lax.rem(lax.div(n, 4), 4), lax.rem(lax.div(n, 2), 2)
    if group == 0:
        both = 2 * lax.div(3 - k, 3) * s
        dy, dz = k * (1 - s) + both, k * s + both
    elif group == 1:
        odd = 1 + 2 * lax.rem(k, 2)
        dy, dz = odd * (1 - s) + 2 * s, 2 * (1 - s) + odd * s
    else:
        dy, dz = 1 + 2 * s, 1 + 2 * lax.rem(s + k, 2)
    return dy, dz, lax.rem(n, 2)


def one_hot(match):
    return match.astype(F32).astype(BF16)


def row_at(n, group):
    return pl.multiple_of(16 * n + (64 if group else 0), 16)


def kernel(owner_hbm, cls_hbm, g_hbm, m_hbm, nm_hbm, up_hbm, own_hbm,
           g, m, nm, zs, zmain, zlo, lor, x, ar1, ar2,
           perm_m, perm_l, back_m, back_l, order, owner_s, cls_s, *rest):
    sums = [rest[3 * i:3 * i + 3] for i in range(3)]
    (gram, t_ref, left, right, coef, u, ulo, vmain, vlo, vl, up, own,
     in_sem, nm_sem, own_sem, up_sem, s1, r1, s2, r2, sm, rm, sl, rl, so, ro, slo, rlo, xs, xr) = rest[9:]
    dp, ex = lax.axis_index("dp"), lax.axis_index("expert")
    y, z, c = dp // 8, (dp // 2) % 4, dp % 2

    def ahead(n, group):
        dy, dz, dc = away(n, group)
        return lax.rem(y + dy, 4) * 8 + lax.rem(z + dz, 4) * 2 + lax.rem(c + dc, 2)

    def behind(n, group):
        dy, dz, dc = away(n, group)
        return lax.rem(y + 4 - dy, 4) * 8 + lax.rem(z + 4 - dz, 4) * 2 + lax.rem(c + dc, 2)

    def each(lo, hi, act):
        for group, (first, end) in enumerate(zip((0,) + GROUPS, GROUPS)):
            if max(lo, first) < min(hi, end):
                def step(n, _, group=group):
                    act(n, group)
                    return _
                lax.fori_loop(max(lo, first), min(hi, end), step, 0)

    per = ROWS // LOADS
    loads = []
    for k in range(LOADS):
        rows = pl.ds(k * per, per)
        for n, (src, dst) in enumerate(((g_hbm, g), (m_hbm, m))):
            cp = pltpu.make_async_copy(src.at[rows], dst.at[rows], in_sem.at[n, k])
            cp.start()
            loads.append(cp)

    tables = [pltpu.make_async_copy(src, dst, up_sem.at[i]) for i, (src, dst) in enumerate(((owner_hbm, owner_s), (cls_hbm, cls_s)))]
    for cp in tables:
        cp.start()
    barrier = pltpu.get_barrier_semaphore()

    each(1, 32, lambda n, group: pl.semaphore_signal(
        barrier, inc=1, device_id=(ahead(n, group), ex), device_id_type=MESH))

    def greet_x(j, _):
        zz, xx = lax.rem(z + lax.rem(j, 4), 4), lax.rem(ex + lax.div(j, 4), 4)
        pl.semaphore_signal(barrier, inc=1, device_id=((y * 4 + zz) * 2 + c, xx), device_id_type=MESH)
        return _
    lax.fori_loop(4, 16, greet_x, 0)

    for cp in tables:
        cp.wait()

    lane = lax.broadcasted_iota(jnp.int32, (8, ROWS), 1)
    mat = lax.broadcasted_iota(jnp.int32, (MATS, 128), 0)
    owner_row = jnp.zeros((8, ROWS), jnp.int32)
    cls = jnp.zeros((MATS, 128), F32)
    for i in range(MATS):
        owner_row = jnp.where(lane % MATS == i, owner_s[i], owner_row)
        cls = jnp.where(mat == i, cls_s[i].astype(F32), cls)
    wanted = (owner_row * RDEV + lane // MATS)[0:1]
    o = lax.broadcasted_iota(jnp.int32, (32, MAIN), 0)
    key = (o // 16) * RDEV + o % 16
    for k in range(16):
        perm_m[32 * k:32 * (k + 1), :] = one_hot(key + 2 * RDEV * k == wanted[:, :MAIN])
    o = lax.broadcasted_iota(jnp.int32, (64, 64), 0)
    perm_l[...] = one_hot((o // 2) * RDEV + 16 + o % 2 == wanted[:, MAIN:])

    def live_at(r):
        return jnp.where(dp * RDEV + r < ROUTER_ROWS, 1.0, 1.0 - cls)

    def rows_of(r):
        return pl.ds(pl.multiple_of(r * MATS, MATS), MATS)

    def stats(r, acc):
        live = live_at(r)
        gg, gm, mm = acc
        for t in range(CDEV // 128):
            cols = slice(t * 128, (t + 1) * 128)
            gv = g[rows_of(r), cols] * live
            mv = m[rows_of(r), cols] * (live * (MU_RATE * MU_RATE))
            gg, gm, mm = gg + gv * gv, gm + gv * mv, mm + mv * mv
        return gg, gm, mm

    acc = (jnp.zeros((MATS, 128), F32),) * 3
    for k in range(LOADS):
        loads[2 * k].wait()
        loads[2 * k + 1].wait()
        acc = lax.fori_loop(k * (RDEV // LOADS), (k + 1) * (RDEV // LOADS), stats, acc)
    tots = [jnp.sum(a, axis=1, keepdims=True) for a in acc]
    col = lax.broadcasted_iota(jnp.int32, (MATS, 128), 1)
    mine = jnp.where(col == 0, tots[0], jnp.where(col == 1, tots[1], jnp.where(col == 2, tots[2], 0.0)))
    mine = jnp.concatenate([mine, jnp.zeros((128 - MATS, 128), F32)], axis=0).T[:8]

    pl.semaphore_wait(barrier, 31 + 12)

    i1, i2 = y * 2 + c, ex * 4 + z
    ar1[i1] = mine

    def got(buf, slot, sem):
        return pltpu.make_async_copy(buf.at[slot], buf.at[slot], sem.at[slot])

    def one_of(j):
        return lax.rem(y + j // 2, 4), lax.rem(c + j % 2, 2)

    def one(j):
        yy, cc = one_of(j)
        return pltpu.make_async_remote_copy(
            src_ref=ar1.at[i1], dst_ref=ar1.at[i1], send_sem=s1.at[j], recv_sem=r1.at[i1],
            device_id=((yy * 4 + z) * 2 + cc, ex), device_id_type=MESH)

    def two_of(j):
        return lax.rem(z + j % 4, 4), lax.rem(ex + j // 4, 4)

    def two(j):
        zz, xx = two_of(j)
        return pltpu.make_async_remote_copy(
            src_ref=ar2.at[i2], dst_ref=ar2.at[i2], send_sem=s2.at[j], recv_sem=r2.at[i2],
            device_id=((y * 4 + zz) * 2 + c, xx), device_id_type=MESH)

    for j in range(1, 8):
        one(j).start()
    for j in range(1, 8):
        yy, cc = one_of(j)
        got(ar1, yy * 2 + cc, r1).wait()
    ar2[i2] = jnp.sum(ar1[...], axis=0)
    for j in range(1, 16):
        two(j).start()
    for j in range(1, 16):
        zz, xx = two_of(j)
        got(ar2, xx * 4 + zz, r2).wait()
    tot = jnp.concatenate([jnp.sum(ar2[...], axis=0), jnp.zeros((120, 128), F32)], axis=0).T[:MATS]
    gg, gm, mm = tot[:, 0:1], tot[:, 1:2], tot[:, 2:3]
    total = jnp.sum(gg, axis=0, keepdims=True)
    clip = jnp.minimum(1.0, jnp.sqrt(float(MATS * ROWS * COLS) / total))
    rate = (1.0 + MU_RATE) * clip
    sq = jnp.where(clip > 0.0, rate * rate * gg + 2.0 * rate * gm, 0.0) + mm
    bound = rate * rate * gg + mm
    faint = jnp.where((clip > 0.0) & (sq < 1e-4 * bound), 1.0, 0.0)
    sq = jnp.where(faint > 0.0, jnp.maximum(sq, 1e-7 * bound), sq)
    divisor = jnp.sqrt(sq) + EPSILON
    inv = jnp.broadcast_to(1.0 / divisor, (MATS, 128))
    clip = jnp.broadcast_to(clip, (MATS, 128))

    def blend(r, _):
        live = live_at(r)
        lc = live * clip
        lm = live * MU_RATE
        for t in range(CDEV // 128):
            cols = slice(t * 128, (t + 1) * 128)
            gv = g[rows_of(r), cols] * lc
            nv = m[rows_of(r), cols] * lm + gv
            nm[rows_of(r), cols] = nv
            zs[rows_of(r), cols] = ((gv + MU_RATE * nv) * inv).astype(BF16)
        return _
    lax.fori_loop(0, RDEV, blend, 0)
    for t in range(CDEV // 256):
        cols = slice(t * 256, (t + 1) * 256)
        zmain[:, cols] = dot(perm_m[...], zs[:MAIN, cols]).astype(BF16)
        zlo[:, :, cols] = dot(perm_l[...], zs[MAIN:, cols]).reshape(MATS, 2, 256).astype(BF16)

    def block(ref, i):
        return ref.at[pl.ds(pl.multiple_of(i * 16, 16), 16)]

    def slot(ref, n, group):
        return ref.at[pl.ds(row_at(n, group), 16)]

    def main_in(n, group):
        to = ahead(n, group)
        return pltpu.make_async_remote_copy(
            src_ref=block(zmain, to), dst_ref=slot(x, n, group), send_sem=sm.at[n], recv_sem=rm.at[group],
            device_id=(to, ex), device_id_type=MESH)

    def lo_in(n, group):
        to = ahead(n, group)
        return pltpu.make_async_remote_copy(
            src_ref=zlo.at[to], dst_ref=lor.at[n], send_sem=sl.at[0], recv_sem=rl.at[0],
            device_id=(to, ex), device_id_type=MESH)

    each(1, 32, lambda n, group: lo_in(n, group).start())
    each(1, WINDOW + 1, lambda n, group: main_in(n, group).start())
    save_nm = pltpu.make_async_copy(nm, nm_hbm, nm_sem)
    save_nm.start()
    x[0:16, :] = zmain[pl.ds(pl.multiple_of(dp * 16, 16), 16), :]
    lor[0] = zlo[dp]

    owner_col = jnp.zeros((MATS, MAIN), jnp.int32)
    mats = lax.broadcasted_iota(jnp.int32, (MATS, MAIN), 0)
    for i in range(MATS):
        owner_col = jnp.where(mats == i, owner_s[i], owner_col)
    here = owner_col[:, :1] == dp
    divisor = jnp.sum(jnp.where(here, divisor, 0.0), axis=0, keepdims=True)
    faint = jnp.sum(jnp.where(here, faint, 0.0), axis=0, keepdims=True)
    owner_col = owner_col * RDEV
    key = ((lane // 16) * RDEV + lane % 16)[0:1, :MAIN]
    for r in range(16):
        back_m[MATS * r:MATS * (r + 1), :] = one_hot(owner_col + r == key)
    key = ((lane // 2) * RDEV + 16 + lane % 2)[0:1, :64]
    for r in range(2):
        back_l[MATS * r:MATS * (r + 1), :] = one_hot(owner_col[:, :64] + (16 + r) == key)
    short = (lane >= SHORT) & (lane < SHORT + 64)
    n = jnp.where(short, (lane - SHORT) // 2, jnp.where(lane < SHORT, lane // 16, lane // 16 - 4))
    source = jnp.where(n < GROUPS[0], behind(n, 0), jnp.where(n < GROUPS[1], behind(n, 1), behind(n, 2)))
    key = (source * RDEV + jnp.where(short, 16 + lane % 2, lane % 16))[0:1]
    for k in range(RDEV):
        rows = lax.broadcasted_iota(jnp.int32, (MATS, ROWS), 0) + MATS * k
        order[MATS * k:MATS * (k + 1), :] = one_hot(rows == key)

    def go(n, group):
        early = n - WINDOW
        main_in(early, 0).wait_send()
        main_in(n, group).start()
    each(WINDOW + 1, GROUPS[0] + WINDOW, go)

    def all_of(ref_at, sem, n=0):
        pltpu.make_async_copy(ref_at, ref_at, sem.at[n]).wait()

    all_of(x.at[pl.ds(16, SHORT - 16)], rm, 0)
    all_of(lor.at[pl.ds(1, MATS - 1)], rl)
    x[SHORT:SHORT + 64, :] = lor[...].astype(F32).reshape(64, CDEV).astype(BF16)

    def put(part, n, piece):
        if piece.shape[1] < 128:
            piece = jnp.concatenate([piece, jnp.zeros((64, 128 - piece.shape[1]), F32)], axis=1)
        part[2 * n] = piece[:32]
        part[2 * n + 1] = piece[32:]

    def terms(i, part):
        low, top = (0,) + TOPS[:2], TOPS[i]
        low = low[i]
        for lo, hi in (((0, 256), (256, top)) if i == 0 else ((0, top),)):
            lo_row = max(low, lo)
            gb = dot_t(x[lo_row:top, :], x[lo:hi, :])
            for n, (r, t) in enumerate(PANELS[i]):
                if lo <= 128 * t < hi:
                    put(part, n, gb[64 * r - lo_row:64 * r - lo_row + 64, 128 * t - lo:min(128 * t + 128, hi) - lo])
        for n in range(2 * len(PANELS[i]), 4 * QUARTERS[i]):
            part[n] = jnp.zeros((32, 128), F32)

    class Sum:
        def __init__(self, part, got, full, size, base):
            self.part, self.got, self.full, self.size, self.base = part, got, full, size, base

        def at(self, xx):
            return pl.ds(xx * self.size, self.size)

        def move(self, src, dst, n, far):
            return pltpu.make_async_remote_copy(
                src_ref=src, dst_ref=dst, send_sem=xs.at[self.base + n], recv_sem=xr.at[self.base + n],
                device_id=(dp, (ex + far) % 4), device_id_type=MESH)

        def scatter(self):
            self.out = [self.move(self.part.at[self.at((ex + far) % 4)], self.got.at[far - 1], far - 1, far) for far in (2, 1, 3)]
            for cp in self.out:
                cp.start()

        def reduce(self):
            for cp in self.out:
                cp.wait_recv()
            here = self.full.at[self.at(ex)]
            self.full[self.at(ex)] = self.part[self.at(ex)] + self.got[0] + (self.got[1] + self.got[2])
            self.back = [self.move(here, here, 2 + far, far) for far in (2, 1, 3)]
            for cp in self.back:
                cp.start()

        def done(self):
            for cp in self.back:
                cp.wait_recv()

        def sent(self):
            for cp in self.out + self.back:
                cp.wait_send()

    def lay_out(i, full):
        for n, (r, t) in enumerate(PANELS[i]):
            w = min(128, TOPS[i] - 128 * t)
            piece = jnp.concatenate([full[2 * n], full[2 * n + 1]], axis=0)
            gram[64 * r:64 * r + 64, 128 * t:128 * t + w] = piece[:, :w]
            if 128 * t + w <= 64 * r:
                gram[128 * t:128 * t + w, 64 * r:64 * r + 64] = piece.T[:w]
            elif 128 * t < 64 * r:
                gram[128 * t:64 * r, 64 * r:64 * r + 64] = piece.T[:64 * r - 128 * t]

    e1, e2, e3 = (Sum(*sums[i], QUARTERS[i], 6 * i) for i in range(3))
    terms(0, e1.part)
    e1.scatter()

    def rest_go(n, group):
        main_in(n - WINDOW, 1).wait_send()
        main_in(n, group).start()
    each(GROUPS[0] + WINDOW, 32, rest_go)
    all_of(x.at[pl.ds(TOPS[0], TOPS[1] - TOPS[0])], rm, 1)
    terms(1, e2.part)
    e2.scatter()
    e1.reduce()
    all_of(x.at[pl.ds(TOPS[1], TOPS[2] - TOPS[1])], rm, 2)
    terms(2, e3.part)
    e3.scatter()
    e2.reduce()
    e1.done()
    lay_out(0, e1.full)
    e3.reduce()
    e2.done()
    lay_out(1, e2.full)
    e3.done()
    lay_out(2, e3.full)

    def symmetric(out, a, b, more=None):
        head = dot(a, b[:, :MAIN])
        corner = dot(a[MAIN:, :], b[:, MAIN:])
        if more is not None:
            head = head + COEF_A * more[:, :MAIN]
            corner = corner + COEF_A * more[MAIN:, MAIN:]
        out[:, :MAIN] = head
        out[MAIN:, MAIN:] = corner
        out[:MAIN, MAIN:] = out[MAIN:, :MAIN].T

    diagonal = lax.broadcasted_iota(jnp.int32, (64, 64), 0) == lax.broadcasted_iota(jnp.int32, (64, 64), 1)
    trace = jnp.zeros((64, 64), F32)
    for r in range(ROWS // 64):
        trace = trace + jnp.where(diagonal, gram[64 * r:64 * r + 64, 64 * r:64 * r + 64], 0.0)
    trace = jnp.sum(jnp.sum(trace, axis=1, keepdims=True), axis=0, keepdims=True)
    fit = jnp.where(faint > 0.0, divisor / (jnp.sqrt(trace) * divisor + EPSILON), 1.0)
    gram[...] = gram[...] * (fit * fit)

    left[:, ROWS:640] = jnp.zeros((ROWS, 64), BF16)
    left[:, 640 + ROWS:] = jnp.zeros((ROWS, 64), BF16)
    right[ROWS:640, :] = jnp.zeros((64, ROWS), BF16)
    right[640 + ROWS:, :] = jnp.zeros((64, ROWS), BF16)
    for k in range(ITERS):
        a16 = gram[...].astype(BF16)
        left[:, :ROWS] = a16
        symmetric(t_ref, left[:, :ROWS], a16)
        b16 = (COEF_B * a16.astype(F32) + COEF_C * t_ref[...]).astype(BF16)
        coef[k] = b16
        if k + 1 < ITERS:
            left[:, 640:640 + ROWS] = (gram[...] - a16.astype(F32)).astype(BF16)
            right[:ROWS, :] = b16
            right[640:640 + ROWS, :] = b16
            t_ref[...] = COEF_A * gram[...] + dot(left[...], right[...])
            left[:, :ROWS] = b16
            left[:, 640:640 + ROWS] = b16
            t16 = t_ref[...].astype(BF16)
            right[:ROWS, :] = t16
            right[640:640 + ROWS, :] = (t_ref[...] - t16.astype(F32)).astype(BF16)
            symmetric(gram, left[...], right[...], t_ref)

    def main_out(p, n, group):
        to = behind(n, group)
        cols = pl.ds(OUT_PARTS[p][0], OUT_PARTS[p][1] - OUT_PARTS[p][0])
        return pltpu.make_async_remote_copy(
            src_ref=u.at[pl.ds(row_at(n, group), 16), cols],
            dst_ref=vmain.at[pl.ds(pl.multiple_of(dp * 16, 16), 16), cols],
            send_sem=so.at[p], recv_sem=ro.at[p], device_id=(to, ex), device_id_type=MESH)

    def lo_out(n, group):
        to = behind(n, group)
        return pltpu.make_async_remote_copy(
            src_ref=ulo.at[n], dst_ref=vlo.at[dp], send_sem=slo.at[0], recv_sem=rlo.at[0],
            device_id=(to, ex), device_id_type=MESH)

    for p, (lo, hi) in enumerate(OUT_PARTS):
        for at in range(lo, hi, 512):
            cols = slice(at, min(at + 512, hi))
            cur = x[:, cols]
            for k in range(ITERS):
                out = COEF_A * cur.astype(F32) + dot(coef[k], cur)
                if k == 0:
                    out = out * fit
                if k + 1 < ITERS:
                    cur = out.astype(BF16)
            res = (SCALE * out).astype(BF16)
            u[:, cols] = res
            ulo[:, :, cols] = res[SHORT:SHORT + 64].astype(F32).reshape(MATS, 2, cols.stop - at).astype(BF16)
        each(1, 32, lambda n, group, p=p: main_out(p, n, group).start())
    each(1, 32, lambda n, group: lo_out(n, group).start())

    vmain[pl.ds(pl.multiple_of(dp * 16, 16), 16), :] = u[0:16, :]
    vlo[dp] = ulo[0]
    for t in range(CDEV // 256):
        cols = slice(t * 256, (t + 1) * 256)
        own[:, cols] = dot(order[...], u[:, cols]).astype(BF16)
    save_own = pltpu.make_async_copy(own, own_hbm, own_sem)
    save_own.start()

    for j in range(1, 8):
        one(j).wait_send()
    for j in range(1, 16):
        two(j).wait_send()
    all_of(zlo.at[pl.ds(0, MATS - 1)], sl)
    each(32 - WINDOW, 32, lambda n, group: main_in(n, group).wait_send())
    for e in (e1, e2, e3):
        e.sent()
    save_nm.wait()

    saves = []
    for p, (lo, hi) in enumerate(OUT_PARTS):
        part_cols = pl.ds(lo, hi - lo)
        all_of(vmain.at[pl.ds(0, MAIN - 16), part_cols], ro, p)
        for at in range(lo, hi, 256):
            cols = slice(at, at + 256)
            up[:MAIN, cols] = dot(back_m[...], vmain[:, cols]).astype(BF16)
        cp = pltpu.make_async_copy(up.at[pl.ds(0, MAIN), part_cols], up_hbm.at[pl.ds(0, MAIN), part_cols], up_sem.at[p])
        cp.start()
        saves.append(cp)
    all_of(vlo.at[pl.ds(0, MATS - 1)], rlo)
    vl[...] = vlo[...].astype(F32).reshape(64, CDEV).astype(BF16)
    up[MAIN:, :] = dot(back_l[...], vl[...]).astype(BF16)
    cp = pltpu.make_async_copy(up.at[pl.ds(MAIN, 64)], up_hbm.at[pl.ds(MAIN, 64)], up_sem.at[len(OUT_PARTS)])
    cp.start()
    saves.append(cp)

    for p, (lo, hi) in enumerate(OUT_PARTS):
        all_of(u.at[pl.ds(0, MAIN - 16), pl.ds(lo, hi - lo)], so, p)
    all_of(ulo.at[pl.ds(0, MATS - 1)], slo)
    save_own.wait()
    for cp in saves:
        cp.wait()


def step(owner, cls, g, m):
    D, V = pltpu.SemaphoreType.DMA, pltpu.VMEM
    wide = (ROWS, CDEV)
    square = (ROWS, ROWS)
    return pl.pallas_call(
        kernel,
        out_shape=(jax.ShapeDtypeStruct(wide, F32), jax.ShapeDtypeStruct(wide, BF16), jax.ShapeDtypeStruct(wide, BF16)),
        in_specs=[pl.BlockSpec(memory_space=pltpu.HBM)] * 4,
        out_specs=(pl.BlockSpec(memory_space=pl.ANY),) * 3,
        scratch_shapes=[
            V(wide, F32), V(wide, F32), V(wide, F32), V(wide, BF16),
            V((MAIN, CDEV), BF16), V((MATS, 2, CDEV), BF16), V((MATS, 2, CDEV), BF16), V(wide, BF16),
            V((8, 8, 128), F32), V((16, 8, 128), F32),
            V((MAIN, MAIN), BF16), V((64, 64), BF16), V((MAIN, MAIN), BF16), V((64, 64), BF16), V(square, BF16),
            pltpu.SMEM((MATS,), jnp.int32), pltpu.SMEM((MATS,), jnp.int32),
            *[V(shape, F32) for q in QUARTERS for shape in ((4 * q, 32, 128), (3, q, 32, 128), (4 * q, 32, 128))],
            V(square, F32), V(square, F32), V((ROWS, 1280), BF16), V((1280, ROWS), BF16), V((ITERS, ROWS, ROWS), BF16),
            V(wide, BF16), V((MATS, 2, CDEV), BF16), V((MAIN, CDEV), BF16), V((MATS, 2, CDEV), BF16), V((64, CDEV), BF16),
            V(wide, BF16), V(wide, BF16),
            D((2, LOADS)), D, D, D((len(OUT_PARTS) + 1,)),
            D((8,)), D((8,)), D((16,)), D((16,)), D((32,)), D((len(GROUPS),)), D((1,)), D((1,)),
            D((len(OUT_PARTS),)), D((len(OUT_PARTS),)), D((1,)), D((1,)), D((18,)), D((18,)),
        ],
        compiler_params=pltpu.CompilerParams(collective_id=0, has_side_effects=True, vmem_limit_bytes=VMEM_LIMIT),
    )(owner, cls, g, m)


def body(gradient, momentum, owner_table, shape_class):
    g = jnp.transpose(gradient, (1, 0, 2)).reshape(ROWS, CDEV)
    m = jnp.transpose(momentum, (1, 0, 2)).reshape(ROWS, CDEV)
    nm, up, own = step(owner_table, shape_class, g, m)
    new_moment = jnp.transpose(nm.reshape(RDEV, MATS, CDEV), (1, 0, 2))
    update = jnp.transpose(up.reshape(RDEV, MATS, CDEV), (1, 0, 2))
    return new_moment, update, own[None]


def solution(mesh):
    return jax.shard_map(
        body,
        mesh=mesh,
        in_specs=(P(None, "dp", "expert"), P(None, "dp", "expert"), P(), P()),
        out_specs=(P(None, "dp", "expert"), P(None, "dp", "expert"), P("dp", None, "expert")),
        check_vma=False,
    )
```

```python
import math

import jax
import jax.numpy as jnp
from jax import lax
from jax.experimental import pallas as pl
from jax.experimental.pallas import tpu as pltpu
from jax.sharding import PartitionSpec as P

MESH = pl.DeviceIdType.MESH
F32, BF16 = jnp.float32, jnp.bfloat16
ROWS, COLS, MATS, RDEV, CDEV = 576, 7168, 32, 18, 1792
ROUTER_ROWS = 384
LOADS = 6
MU_RATE, EPSILON = 0.95, 1e-07
COEF_A, COEF_B, COEF_C, ITERS = 3.4445, -4.775, 2.0315, 4
SCALE = 0.2 * math.sqrt(COLS)
VMEM_LIMIT = 44 * 1024 * 1024
MAIN = 512
OUT_PARTS = ((0, 256), (256, 768), (768, CDEV))
WINDOW = 12
GROUPS = (16, 24, 32)
SHORT = 16 * GROUPS[0]
TOPS = (SHORT + 64, 16 * GROUPS[1] + 64, ROWS)
PANELS = tuple(tuple((r, t) for r in range(lo // 64, hi // 64) for t in range(r // 2 + 1))
               for lo, hi in zip((0,) + TOPS, TOPS))
QUARTERS = tuple(-(-2 * len(p) // 4) for p in PANELS)


def dot(a, b):
    return jnp.dot(a, b, preferred_element_type=F32)


def dot_t(a, b):
    return lax.dot_general(a, b, (((1,), (1,)), ((), ())), preferred_element_type=F32)


def away(n, group):
    k, s = lax.rem(lax.div(n, 4), 4), lax.rem(lax.div(n, 2), 2)
    if group == 0:
        both = 2 * lax.div(3 - k, 3) * s
        dy, dz = k * (1 - s) + both, k * s + both
    elif group == 1:
        odd = 1 + 2 * lax.rem(k, 2)
        dy, dz = odd * (1 - s) + 2 * s, 2 * (1 - s) + odd * s
    else:
        dy, dz = 1 + 2 * s, 1 + 2 * lax.rem(s + k, 2)
    return dy, dz, lax.rem(n, 2)


def one_hot(match):
    return match.astype(F32).astype(BF16)


def row_at(n, group):
    return pl.multiple_of(16 * n + (64 if group else 0), 16)


def kernel(owner_hbm, cls_hbm, g_hbm, m_hbm, nm_hbm, up_hbm, own_hbm,
           g, m, nm, zs, zmain, zlo, lor, x, ar1, ar2,
           perm_m, perm_l, back_m, back_l, order, owner_s, cls_s, *rest):
    sums = [rest[3 * i:3 * i + 3] for i in range(3)]
    (gram, t_ref, left, right, coef, u, ulo, vmain, vlo, vl, up, own,
     in_sem, nm_sem, own_sem, up_sem, s1, r1, s2, r2, sm, rm, sl, rl, so, ro, slo, rlo, xs, xr) = rest[9:]
    dp, ex = lax.axis_index("dp"), lax.axis_index("expert")
    y, z, c = dp // 8, (dp // 2) % 4, dp % 2

    def ahead(n, group):
        dy, dz, dc = away(n, group)
        return lax.rem(y + dy, 4) * 8 + lax.rem(z + dz, 4) * 2 + lax.rem(c + dc, 2)

    def behind(n, group):
        dy, dz, dc = away(n, group)
        return lax.rem(y + 4 - dy, 4) * 8 + lax.rem(z + 4 - dz, 4) * 2 + lax.rem(c + dc, 2)

    def each(lo, hi, act):
        for group, (first, end) in enumerate(zip((0,) + GROUPS, GROUPS)):
            if max(lo, first) < min(hi, end):
                def step(n, _, group=group):
                    act(n, group)
                    return _
                lax.fori_loop(max(lo, first), min(hi, end), step, 0)

    barrier = pltpu.get_barrier_semaphore()
    each(1, 32, lambda n, group: pl.semaphore_signal(
        barrier, inc=1, device_id=(ahead(n, group), ex), device_id_type=MESH))

    def greet_x(j, _):
        zz, xx = lax.rem(z + lax.rem(j, 4), 4), lax.rem(ex + lax.div(j, 4), 4)
        pl.semaphore_signal(barrier, inc=1, device_id=((y * 4 + zz) * 2 + c, xx), device_id_type=MESH)
        return _
    lax.fori_loop(4, 16, greet_x, 0)

    per = ROWS // LOADS
    loads = []
    for k in range(LOADS):
        rows = pl.ds(k * per, per)
        for n, (src, dst) in enumerate(((g_hbm, g), (m_hbm, m))):
            cp = pltpu.make_async_copy(src.at[rows], dst.at[rows], in_sem.at[n, k])
            cp.start()
            loads.append(cp)
    tables = [pltpu.make_async_copy(src, dst, up_sem.at[i]) for i, (src, dst) in enumerate(((owner_hbm, owner_s), (cls_hbm, cls_s)))]
    for cp in tables:
        cp.start()

    for cp in tables:
        cp.wait()

    lane = lax.broadcasted_iota(jnp.int32, (8, ROWS), 1)
    mat = lax.broadcasted_iota(jnp.int32, (MATS, 128), 0)
    owner_row = jnp.zeros((8, ROWS), jnp.int32)
    cls = jnp.zeros((MATS, 128), F32)
    for i in range(MATS):
        owner_row = jnp.where(lane % MATS == i, owner_s[i], owner_row)
        cls = jnp.where(mat == i, cls_s[i].astype(F32), cls)
    wanted = (owner_row * RDEV + lane // MATS)[0:1]
    o = lax.broadcasted_iota(jnp.int32, (32, MAIN), 0)
    key = (o // 16) * RDEV + o % 16
    for k in range(16):
        perm_m[32 * k:32 * (k + 1), :] = one_hot(key + 2 * RDEV * k == wanted[:, :MAIN])
    o = lax.broadcasted_iota(jnp.int32, (64, 64), 0)
    perm_l[...] = one_hot((o // 2) * RDEV + 16 + o % 2 == wanted[:, MAIN:])

    def live_at(r):
        return jnp.where(dp * RDEV + r < ROUTER_ROWS, 1.0, 1.0 - cls)

    def rows_of(r):
        return pl.ds(pl.multiple_of(r * MATS, MATS), MATS)

    def stats(r, acc):
        live = live_at(r)
        gg, gm, mm = acc
        for t in range(CDEV // 128):
            cols = slice(t * 128, (t + 1) * 128)
            gv = g[rows_of(r), cols] * live
            mv = m[rows_of(r), cols] * (live * (MU_RATE * MU_RATE))
            gg, gm, mm = gg + gv * gv, gm + gv * mv, mm + mv * mv
        return gg, gm, mm

    acc = (jnp.zeros((MATS, 128), F32),) * 3
    for k in range(LOADS):
        loads[2 * k].wait()
        loads[2 * k + 1].wait()
        acc = lax.fori_loop(k * (RDEV // LOADS), (k + 1) * (RDEV // LOADS), stats, acc)
    tots = [jnp.sum(a, axis=1, keepdims=True) for a in acc]
    col = lax.broadcasted_iota(jnp.int32, (MATS, 128), 1)
    mine = jnp.where(col == 0, tots[0], jnp.where(col == 1, tots[1], jnp.where(col == 2, tots[2], 0.0)))
    mine = jnp.concatenate([mine, jnp.zeros((128 - MATS, 128), F32)], axis=0).T[:8]

    pl.semaphore_wait(barrier, 31 + 12)

    i1, i2 = y * 2 + c, ex * 4 + z
    ar1[i1] = mine

    def all_of(ref_at, sem, n=0):
        pltpu.make_async_copy(ref_at, ref_at, sem.at[n]).wait()

    def one_of(j):
        return lax.rem(y + j // 2, 4), lax.rem(c + j % 2, 2)

    def one(j):
        yy, cc = one_of(j)
        return pltpu.make_async_remote_copy(
            src_ref=ar1.at[i1], dst_ref=ar1.at[i1], send_sem=s1.at[j], recv_sem=r1.at[0],
            device_id=((yy * 4 + z) * 2 + cc, ex), device_id_type=MESH)

    def two_of(j):
        return lax.rem(z + j % 4, 4), lax.rem(ex + j // 4, 4)

    def two(j):
        zz, xx = two_of(j)
        return pltpu.make_async_remote_copy(
            src_ref=ar2.at[i2], dst_ref=ar2.at[i2], send_sem=s2.at[j], recv_sem=r2.at[0],
            device_id=((y * 4 + zz) * 2 + c, xx), device_id_type=MESH)

    for j in range(1, 8):
        one(j).start()
    all_of(ar1.at[pl.ds(0, 7)], r1)
    ar2[i2] = jnp.sum(ar1[...], axis=0)
    for j in range(1, 16):
        two(j).start()
    all_of(ar2.at[pl.ds(0, 15)], r2)
    tot = jnp.concatenate([jnp.sum(ar2[...], axis=0), jnp.zeros((120, 128), F32)], axis=0).T[:MATS]
    gg, gm, mm = tot[:, 0:1], tot[:, 1:2], tot[:, 2:3]
    total = jnp.sum(gg, axis=0, keepdims=True)
    clip = jnp.minimum(1.0, jnp.sqrt(float(MATS * ROWS * COLS) / total))
    rate = (1.0 + MU_RATE) * clip
    sq = jnp.where(clip > 0.0, rate * rate * gg + 2.0 * rate * gm, 0.0) + mm
    bound = rate * rate * gg + mm
    faint = jnp.where((clip > 0.0) & (sq < 1e-4 * bound), 1.0, 0.0)
    sq = jnp.where(faint > 0.0, jnp.maximum(sq, 1e-7 * bound), sq)
    divisor = jnp.sqrt(sq) + EPSILON
    inv = jnp.broadcast_to(1.0 / divisor, (MATS, 128))
    clip = jnp.broadcast_to(clip, (MATS, 128))

    def blend(r, _):
        live = live_at(r)
        lc = live * clip
        lm = live * MU_RATE
        for t in range(CDEV // 128):
            cols = slice(t * 128, (t + 1) * 128)
            gv = g[rows_of(r), cols] * lc
            nv = m[rows_of(r), cols] * lm + gv
            nm[rows_of(r), cols] = nv
            zs[rows_of(r), cols] = ((gv + MU_RATE * nv) * inv).astype(BF16)
        return _
    lax.fori_loop(0, RDEV, blend, 0)
    for t in range(CDEV // 256):
        cols = slice(t * 256, (t + 1) * 256)
        zmain[:, cols] = dot(perm_m[...], zs[:MAIN, cols]).astype(BF16)
        zlo[:, :, cols] = dot(perm_l[...], zs[MAIN:, cols]).reshape(MATS, 2, 256).astype(BF16)

    def block(ref, i):
        return ref.at[pl.ds(pl.multiple_of(i * 16, 16), 16)]

    def slot(ref, n, group):
        return ref.at[pl.ds(row_at(n, group), 16)]

    def main_in(n, group):
        to = ahead(n, group)
        return pltpu.make_async_remote_copy(
            src_ref=block(zmain, to), dst_ref=slot(x, n, group), send_sem=sm.at[n], recv_sem=rm.at[group],
            device_id=(to, ex), device_id_type=MESH)

    def lo_in(n, group):
        to = ahead(n, group)
        return pltpu.make_async_remote_copy(
            src_ref=zlo.at[to], dst_ref=lor.at[n], send_sem=sl.at[0], recv_sem=rl.at[0],
            device_id=(to, ex), device_id_type=MESH)

    each(1, WINDOW + 1, lambda n, group: main_in(n, group).start())
    each(1, 32, lambda n, group: lo_in(n, group).start())
    save_nm = pltpu.make_async_copy(nm, nm_hbm, nm_sem)
    save_nm.start()
    x[0:16, :] = zmain[pl.ds(pl.multiple_of(dp * 16, 16), 16), :]
    lor[0] = zlo[dp]

    owner_col = jnp.zeros((MATS, MAIN), jnp.int32)
    mats = lax.broadcasted_iota(jnp.int32, (MATS, MAIN), 0)
    for i in range(MATS):
        owner_col = jnp.where(mats == i, owner_s[i], owner_col)
    here = owner_col[:, :1] == dp
    divisor = jnp.sum(jnp.where(here, divisor, 0.0), axis=0, keepdims=True)
    faint = jnp.sum(jnp.where(here, faint, 0.0), axis=0, keepdims=True)
    owner_col = owner_col * RDEV
    key = ((lane // 16) * RDEV + lane % 16)[0:1, :MAIN]
    for r in range(16):
        back_m[MATS * r:MATS * (r + 1), :] = one_hot(owner_col + r == key)
    key = ((lane // 2) * RDEV + 16 + lane % 2)[0:1, :64]
    for r in range(2):
        back_l[MATS * r:MATS * (r + 1), :] = one_hot(owner_col[:, :64] + (16 + r) == key)
    short = (lane >= SHORT) & (lane < SHORT + 64)
    n = jnp.where(short, (lane - SHORT) // 2, jnp.where(lane < SHORT, lane // 16, lane // 16 - 4))
    source = jnp.where(n < GROUPS[0], behind(n, 0), jnp.where(n < GROUPS[1], behind(n, 1), behind(n, 2)))
    key = (source * RDEV + jnp.where(short, 16 + lane % 2, lane % 16))[0:1]
    for k in range(RDEV):
        rows = lax.broadcasted_iota(jnp.int32, (MATS, ROWS), 0) + MATS * k
        order[MATS * k:MATS * (k + 1), :] = one_hot(rows == key)

    def go(n, group):
        early = n - WINDOW
        main_in(early, 0).wait_send()
        main_in(n, group).start()
    each(WINDOW + 1, GROUPS[0] + WINDOW, go)

    all_of(x.at[pl.ds(16, SHORT - 16)], rm, 0)
    all_of(lor.at[pl.ds(1, MATS - 1)], rl)
    x[SHORT:SHORT + 64, :] = lor[...].astype(F32).reshape(64, CDEV).astype(BF16)

    def put(part, n, piece):
        if piece.shape[1] < 128:
            piece = jnp.concatenate([piece, jnp.zeros((64, 128 - piece.shape[1]), F32)], axis=1)
        part[2 * n] = piece[:32]
        part[2 * n + 1] = piece[32:]

    def terms(i, part):
        low, top = (0,) + TOPS[:2], TOPS[i]
        low = low[i]
        for lo, hi in (((0, 256), (256, top)) if i == 0 else ((0, top),)):
            lo_row = max(low, lo)
            gb = dot_t(x[lo_row:top, :], x[lo:hi, :])
            for n, (r, t) in enumerate(PANELS[i]):
                if lo <= 128 * t < hi:
                    put(part, n, gb[64 * r - lo_row:64 * r - lo_row + 64, 128 * t - lo:min(128 * t + 128, hi) - lo])
        for n in range(2 * len(PANELS[i]), 4 * QUARTERS[i]):
            part[n] = jnp.zeros((32, 128), F32)

    class Sum:
        def __init__(self, part, got, full, size, base):
            self.part, self.got, self.full, self.size, self.base = part, got, full, size, base

        def at(self, xx):
            return pl.ds(xx * self.size, self.size)

        def move(self, src, dst, n, far):
            return pltpu.make_async_remote_copy(
                src_ref=src, dst_ref=dst, send_sem=xs.at[self.base + n], recv_sem=xr.at[self.base + n],
                device_id=(dp, (ex + far) % 4), device_id_type=MESH)

        def scatter(self):
            self.out = [self.move(self.part.at[self.at((ex + far) % 4)], self.got.at[far - 1], far - 1, far) for far in (2, 1, 3)]
            for cp in self.out:
                cp.start()

        def reduce(self):
            for cp in self.out:
                cp.wait_recv()
            here = self.full.at[self.at(ex)]
            self.full[self.at(ex)] = self.part[self.at(ex)] + self.got[0] + (self.got[1] + self.got[2])
            self.back = [self.move(here, here, 2 + far, far) for far in (2, 1, 3)]
            for cp in self.back:
                cp.start()

        def done(self):
            for cp in self.back:
                cp.wait_recv()

        def sent(self):
            for cp in self.out + self.back:
                cp.wait_send()

    def lay_out(i, full):
        for n, (r, t) in enumerate(PANELS[i]):
            w = min(128, TOPS[i] - 128 * t)
            piece = jnp.concatenate([full[2 * n], full[2 * n + 1]], axis=0)
            gram[64 * r:64 * r + 64, 128 * t:128 * t + w] = piece[:, :w]
            if 128 * t + w <= 64 * r:
                gram[128 * t:128 * t + w, 64 * r:64 * r + 64] = piece.T[:w]
            elif 128 * t < 64 * r:
                gram[128 * t:64 * r, 64 * r:64 * r + 64] = piece.T[:64 * r - 128 * t]

    e1, e2, e3 = (Sum(*sums[i], QUARTERS[i], 6 * i) for i in range(3))
    terms(0, e1.part)
    e1.scatter()

    def rest_go(n, group):
        main_in(n - WINDOW, 1).wait_send()
        main_in(n, group).start()
    each(GROUPS[0] + WINDOW, 32, rest_go)
    all_of(x.at[pl.ds(TOPS[0], TOPS[1] - TOPS[0])], rm, 1)
    terms(1, e2.part)
    e2.scatter()
    e1.reduce()
    all_of(x.at[pl.ds(TOPS[1], TOPS[2] - TOPS[1])], rm, 2)
    terms(2, e3.part)
    e3.scatter()
    e2.reduce()
    e1.done()
    lay_out(0, e1.full)
    e3.reduce()
    e2.done()
    lay_out(1, e2.full)
    e3.done()
    lay_out(2, e3.full)

    def symmetric(out, a, b, more=None):
        head = dot(a, b[:, :MAIN])
        corner = dot(a[MAIN:, :], b[:, MAIN:])
        if more is not None:
            head = head + COEF_A * more[:, :MAIN]
            corner = corner + COEF_A * more[MAIN:, MAIN:]
        out[:, :MAIN] = head
        out[MAIN:, MAIN:] = corner
        out[:MAIN, MAIN:] = out[MAIN:, :MAIN].T

    diagonal = lax.broadcasted_iota(jnp.int32, (64, 64), 0) == lax.broadcasted_iota(jnp.int32, (64, 64), 1)
    trace = jnp.zeros((64, 64), F32)
    for r in range(ROWS // 64):
        trace = trace + jnp.where(diagonal, gram[64 * r:64 * r + 64, 64 * r:64 * r + 64], 0.0)
    trace = jnp.sum(jnp.sum(trace, axis=1, keepdims=True), axis=0, keepdims=True)
    fit = jnp.where(faint > 0.0, divisor / (jnp.sqrt(trace) * divisor + EPSILON), 1.0)
    gram[...] = gram[...] * (fit * fit)

    left[:, ROWS:640] = jnp.zeros((ROWS, 64), BF16)
    left[:, 640 + ROWS:] = jnp.zeros((ROWS, 64), BF16)
    right[ROWS:640, :] = jnp.zeros((64, ROWS), BF16)
    right[640 + ROWS:, :] = jnp.zeros((64, ROWS), BF16)
    for k in range(ITERS):
        a16 = gram[...].astype(BF16)
        left[:, :ROWS] = a16
        symmetric(t_ref, left[:, :ROWS], a16)
        b16 = (COEF_B * a16.astype(F32) + COEF_C * t_ref[...]).astype(BF16)
        coef[k] = b16
        if k + 1 < ITERS:
            left[:, 640:640 + ROWS] = (gram[...] - a16.astype(F32)).astype(BF16)
            right[:ROWS, :] = b16
            right[640:640 + ROWS, :] = b16
            t_ref[...] = COEF_A * gram[...] + dot(left[...], right[...])
            left[:, :ROWS] = b16
            left[:, 640:640 + ROWS] = b16
            t16 = t_ref[...].astype(BF16)
            right[:ROWS, :] = t16
            right[640:640 + ROWS, :] = (t_ref[...] - t16.astype(F32)).astype(BF16)
            symmetric(gram, left[...], right[...], t_ref)

    def main_out(p, n, group):
        to = behind(n, group)
        cols = pl.ds(OUT_PARTS[p][0], OUT_PARTS[p][1] - OUT_PARTS[p][0])
        return pltpu.make_async_remote_copy(
            src_ref=u.at[pl.ds(row_at(n, group), 16), cols],
            dst_ref=vmain.at[pl.ds(pl.multiple_of(dp * 16, 16), 16), cols],
            send_sem=so.at[p], recv_sem=ro.at[p], device_id=(to, ex), device_id_type=MESH)

    def lo_out(n, group):
        to = behind(n, group)
        return pltpu.make_async_remote_copy(
            src_ref=ulo.at[n], dst_ref=vlo.at[dp], send_sem=slo.at[0], recv_sem=rlo.at[0],
            device_id=(to, ex), device_id_type=MESH)

    for p, (lo, hi) in enumerate(OUT_PARTS):
        for at in range(lo, hi, 512):
            cols = slice(at, min(at + 512, hi))
            cur = x[:, cols]
            for k in range(ITERS):
                out = COEF_A * cur.astype(F32) + dot(coef[k], cur)
                if k == 0:
                    out = out * fit
                if k + 1 < ITERS:
                    cur = out.astype(BF16)
            res = (SCALE * out).astype(BF16)
            u[:, cols] = res
            ulo[:, :, cols] = res[SHORT:SHORT + 64].astype(F32).reshape(MATS, 2, cols.stop - at).astype(BF16)
        each(1, 32, lambda n, group, p=p: main_out(p, n, group).start())
    each(1, 32, lambda n, group: lo_out(n, group).start())

    vmain[pl.ds(pl.multiple_of(dp * 16, 16), 16), :] = u[0:16, :]
    vlo[dp] = ulo[0]
    for t in range(CDEV // 256):
        cols = slice(t * 256, (t + 1) * 256)
        own[:, cols] = dot(order[...], u[:, cols]).astype(BF16)
    save_own = pltpu.make_async_copy(own, own_hbm, own_sem)
    save_own.start()

    for j in range(1, 8):
        one(j).wait_send()
    for j in range(1, 16):
        two(j).wait_send()
    all_of(zlo.at[pl.ds(0, MATS - 1)], sl)
    each(32 - WINDOW, 32, lambda n, group: main_in(n, group).wait_send())
    for e in (e1, e2, e3):
        e.sent()
    save_nm.wait()

    saves = []
    for p, (lo, hi) in enumerate(OUT_PARTS):
        part_cols = pl.ds(lo, hi - lo)
        all_of(vmain.at[pl.ds(0, MAIN - 16), part_cols], ro, p)
        for at in range(lo, hi, 256):
            cols = slice(at, at + 256)
            up[:MAIN, cols] = dot(back_m[...], vmain[:, cols]).astype(BF16)
        cp = pltpu.make_async_copy(up.at[pl.ds(0, MAIN), part_cols], up_hbm.at[pl.ds(0, MAIN), part_cols], up_sem.at[p])
        cp.start()
        saves.append(cp)
    all_of(vlo.at[pl.ds(0, MATS - 1)], rlo)
    vl[...] = vlo[...].astype(F32).reshape(64, CDEV).astype(BF16)
    up[MAIN:, :] = dot(back_l[...], vl[...]).astype(BF16)
    cp = pltpu.make_async_copy(up.at[pl.ds(MAIN, 64)], up_hbm.at[pl.ds(MAIN, 64)], up_sem.at[len(OUT_PARTS)])
    cp.start()
    saves.append(cp)

    for p, (lo, hi) in enumerate(OUT_PARTS):
        all_of(u.at[pl.ds(0, MAIN - 16), pl.ds(lo, hi - lo)], so, p)
    all_of(ulo.at[pl.ds(0, MATS - 1)], slo)
    save_own.wait()
    for cp in saves:
        cp.wait()


def step(owner, cls, g, m):
    D, V = pltpu.SemaphoreType.DMA, pltpu.VMEM
    wide = (ROWS, CDEV)
    square = (ROWS, ROWS)
    return pl.pallas_call(
        kernel,
        out_shape=(jax.ShapeDtypeStruct(wide, F32), jax.ShapeDtypeStruct(wide, BF16), jax.ShapeDtypeStruct(wide, BF16)),
        in_specs=[pl.BlockSpec(memory_space=pltpu.HBM)] * 4,
        out_specs=(pl.BlockSpec(memory_space=pl.ANY),) * 3,
        scratch_shapes=[
            V(wide, F32), V(wide, F32), V(wide, F32), V(wide, BF16),
            V((MAIN, CDEV), BF16), V((MATS, 2, CDEV), BF16), V((MATS, 2, CDEV), BF16), V(wide, BF16),
            V((8, 8, 128), F32), V((16, 8, 128), F32),
            V((MAIN, MAIN), BF16), V((64, 64), BF16), V((MAIN, MAIN), BF16), V((64, 64), BF16), V(square, BF16),
            pltpu.SMEM((MATS,), jnp.int32), pltpu.SMEM((MATS,), jnp.int32),
            *[V(shape, F32) for q in QUARTERS for shape in ((4 * q, 32, 128), (3, q, 32, 128), (4 * q, 32, 128))],
            V(square, F32), V(square, F32), V((ROWS, 1280), BF16), V((1280, ROWS), BF16), V((ITERS, ROWS, ROWS), BF16),
            V(wide, BF16), V((MATS, 2, CDEV), BF16), V((MAIN, CDEV), BF16), V((MATS, 2, CDEV), BF16), V((64, CDEV), BF16),
            V(wide, BF16), V(wide, BF16),
            D((2, LOADS)), D, D, D((len(OUT_PARTS) + 1,)),
            D((8,)), D((1,)), D((16,)), D((1,)), D((32,)), D((len(GROUPS),)), D((1,)), D((1,)),
            D((len(OUT_PARTS),)), D((len(OUT_PARTS),)), D((1,)), D((1,)), D((18,)), D((18,)),
        ],
        compiler_params=pltpu.CompilerParams(collective_id=0, has_side_effects=True, vmem_limit_bytes=VMEM_LIMIT),
    )(owner, cls, g, m)


def body(gradient, momentum, owner_table, shape_class):
    g = jnp.transpose(gradient, (1, 0, 2)).reshape(ROWS, CDEV)
    m = jnp.transpose(momentum, (1, 0, 2)).reshape(ROWS, CDEV)
    nm, up, own = step(owner_table, shape_class, g, m)
    new_moment = jnp.transpose(nm.reshape(RDEV, MATS, CDEV), (1, 0, 2))
    update = jnp.transpose(up.reshape(RDEV, MATS, CDEV), (1, 0, 2))
    return new_moment, update, own[None]


def solution(mesh):
    return jax.shard_map(
        body,
        mesh=mesh,
        in_specs=(P(None, "dp", "expert"), P(None, "dp", "expert"), P(), P()),
        out_specs=(P(None, "dp", "expert"), P(None, "dp", "expert"), P("dp", None, "expert")),
        check_vma=False,
    )
```
